128 devices in a mesh: py: 8 (over z, core), px: 16 (over x, y).
Axes of the slice: x: 4, y: 4, z: 4, core: 2. Of those that a mesh axis runs over, the one named last changes fastest.
Arguments:
- features: bfloat16 [512, 2048, 256], P('py', 'px'), may hold values from -6 to 6
- coarse: bfloat16 [1024, 100, 128], P(('py', 'px')), may hold values from -6 to 6
- send_ids: int32 [128, 128, 2], P(('py', 'px')), may hold values from 0 to 7, as said below
- send_counts: int32 [128, 128], P(('py', 'px')), may hold values from 0 to 2, as said below
- entry_slot: int32 [128, 256], P(('py', 'px')), may hold values from 0 to 255, as said below
- entry_weight_pattern: int32 [128, 256], P(('py', 'px')), may hold values from 0 to 7
- interpolation_weights: bfloat16 [8, 128, 128], replicated, may hold values from -0.25 to 0.25
- lift_weight: bfloat16 [100, 256], replicated, may hold values from -0.625 to 0.625
- conv_a: bfloat16 [3, 3, 256, 256], replicated, may hold values from -0.125 to 0.125
- conv_b: bfloat16 [3, 3, 256, 512], replicated, may hold values from -0.125 to 0.125
- up_weight: bfloat16 [512, 256], replicated, may hold values from -0.25 to 0.25
Outputs:
- output: bfloat16 [512, 2048, 256], P('py', 'px')
The draws below stay inside these ranges and needn't reach their ends.
Inputs may be any that keep to these rules, and one draw needn't show every extreme that they name: send_ids[s, p, k] is the local index, on owner s, of the k-th block that s sends to patch p; the first send_counts[s, p] of them are distinct. send_counts[s, p] blocks go from owner s to patch p; send_counts[p, p] = 2. entry_slot[p, e] = s * 2 + k names the k-th block sent by owner s to patch p, with k < send_counts[s, p]; every block sent to patch p is named by some entry of p.
All inputs are finite; a program needn't handle non-finite values.
Results may differ from the reference program's by a relative error of at most 0.013.
Values may be sent and summed in bfloat16 or wider, within the bound.
No kernel may reach another device: no remote copies, remote signals or barrier semaphores. Data moves between devices by JAX's collectives and lax.ppermute only.
A program may use at most 256 MiB of HBM per device.

```python
import jax
import jax.numpy as jnp
from jax import lax

C0 = 100
FINE_CHANNELS = 256
CB = 512
BLK = 128
BLK_DEV = 8
CAP = 2
NW = 8
SUBTILE_ENTRIES = 4
SUBTILE_ROWS = 8
SUBTILE_COLUMNS = 16
PATCH_ROWS = 64
PATCH_COLUMNS = 128
SUBPIX = 128
NSUB = 64
NENT = 256
NBLK = 1024
GH = 512
GW = 2048
N_PY = 8
N_PX = 16
DEVICES = 128


def route_plan(key):
    first_key, second_key, third_key = jax.random.split(key, 3)
    popular = jax.random.randint(first_key, (DEVICES, 1), 0, 4) == 0
    heavy = jnp.minimum(jax.random.randint(second_key, (DEVICES, DEVICES), 1, CAP + 2), CAP)
    light = jnp.minimum(jax.random.randint(third_key, (DEVICES, DEVICES), 0, 3), CAP)
    raw = jnp.where(popular, heavy, light)
    diagonal = jnp.arange(DEVICES)[:, None] == jnp.arange(DEVICES)[None, :]
    offdiag = jnp.where(diagonal, 0, raw)
    before = jnp.cumsum(offdiag, axis=0) - offdiag
    offdiag = jnp.minimum(offdiag, jnp.maximum(NENT - CAP - before, 0))
    return jnp.where(diagonal, CAP, offdiag).astype(jnp.int32)


def draw_send_counts(key, part):
    return route_plan(key)


def draw_send_ids(key, part):
    key = jax.random.fold_in(key, 11)
    scores = jax.random.randint(key, (DEVICES, DEVICES, BLK_DEV), 0, 2 ** 20)
    scores = scores * BLK_DEV + jnp.arange(BLK_DEV, dtype=jnp.int32)[None, None, :]
    order = jnp.argsort(scores, axis=-1, stable=True)
    return order[:, :, :CAP].astype(jnp.int32)


def draw_entry_slot(key, part):
    counts = route_plan(key)
    key = jax.random.fold_in(key, 23)
    pick_key, order_key = jax.random.split(key)
    place = jnp.arange(DEVICES * CAP, dtype=jnp.int32) % CAP
    source = jnp.arange(DEVICES * CAP, dtype=jnp.int32) // CAP
    valid = (place[None, :] < counts[source, :].T).astype(jnp.int32)
    received = jnp.sum(valid, axis=1)
    order = jnp.argsort(1 - valid, axis=1, stable=True).astype(jnp.int32)
    extra = jax.random.randint(pick_key, (DEVICES, NENT), 0, 2 ** 20) % received[:, None]
    position = jnp.arange(NENT, dtype=jnp.int32)[None, :]
    index = jnp.where(position < received[:, None], position, extra)
    slots = jnp.take_along_axis(order, index, axis=1)
    mixing = jax.random.randint(order_key, (DEVICES, NENT), 0, 2 ** 16) * NENT + position
    permuted = jnp.argsort(mixing, axis=1, stable=True)
    return jnp.take_along_axis(slots, permuted, axis=1).astype(jnp.int32)


def with_ends(drawn, key, low, top_value):
    longest = drawn.shape.index(max(drawn.shape))
    spots = []
    for shift in (0, 1):
        where = [jax.random.randint(jax.random.fold_in(key, axis), (), 0, length) for axis, length in enumerate(drawn.shape)]
        where[longest] = (where[longest] + shift) % drawn.shape[longest]
        spots.append(tuple(where))
    return drawn.at[spots[0]].set(low).at[spots[1]].set(top_value)


def steps_of(stream_key, dims, shards, low, largest):
    loudness = 1.0
    for axis_at, parts in shards:
        heights = jax.random.uniform(jax.random.fold_in(jax.random.fold_in(stream_key, 6), axis_at), (parts,), jnp.float32, low / len(shards), largest / len(shards))
        loudness = loudness * jnp.repeat(jnp.exp(heights), dims[axis_at] // parts).reshape((-1,) + (1,) * (len(dims) - 1 - axis_at))
    return loudness


def bell_draw(key, extent, scale, reach, cuts=(), kind=jnp.bfloat16):
    factor_of = steps_of(key, extent, cuts, -0.22, 0.18) if cuts else 1.0
    array = jax.random.normal(key, extent, jnp.float32) * scale * factor_of
    return jnp.minimum(jnp.maximum(array, -reach), reach).astype(kind)


def setup_inputs(seed: int = 0) -> dict:
    splits = jax.random.split(jax.random.key(seed), 12)
    return {
        "features": bell_draw(splits[0], (GH, GW, FINE_CHANNELS), 1.0, 6.0, ((0, 8), (1, 16))),
        "coarse": bell_draw(splits[1], (NBLK, C0, BLK), 1.0, 6.0, ((0, 128),)),
        "send_ids": draw_send_ids(jax.random.fold_in(splits[11], 71), 0),
        "send_counts": draw_send_counts(jax.random.fold_in(splits[11], 71), 0),
        "entry_slot": draw_entry_slot(jax.random.fold_in(splits[11], 71), 0),
        "entry_weight_pattern": with_ends(jax.random.randint(splits[5], (DEVICES, NENT), 0, NW), jax.random.fold_in(splits[5], 1), 0, NW - 1).astype(jnp.int32),
        "interpolation_weights": bell_draw(splits[6], (NW, BLK, SUBPIX), (SUBTILE_ENTRIES * BLK) ** -0.5, 0.25),
        "lift_weight": bell_draw(splits[7], (C0, FINE_CHANNELS), C0 ** -0.5, 0.625),
        "conv_a": bell_draw(splits[8], (3, 3, FINE_CHANNELS, FINE_CHANNELS), (9 * FINE_CHANNELS) ** -0.5, 0.125),
        "conv_b": bell_draw(splits[9], (3, 3, FINE_CHANNELS, CB), (9 * FINE_CHANNELS) ** -0.5, 0.125),
        "up_weight": bell_draw(splits[10], (CB, FINE_CHANNELS), CB ** -0.5, 0.25),
    }


def conv_three(grid, kernel):
    row_count = grid.shape[0]
    column_count = grid.shape[1]
    padded = jnp.pad(grid, ((1, 1), (1, 1), (0, 0)))
    total = jnp.zeros((row_count, column_count, kernel.shape[3]), jnp.float32)
    for row_off in range(3):
        for col_off in range(3):
            total = total + jnp.dot(padded[row_off:row_off + row_count, col_off:col_off + column_count], kernel[row_off, col_off], preferred_element_type=jnp.float32)
    return total


def reference(features, coarse, send_ids, send_counts, entry_slot, entry_weight_pattern, interpolation_weights, lift_weight, conv_a, conv_b, up_weight):
    lift_wide = lift_weight.astype(jnp.float32)

    def one_patch(patch):
        slots = entry_slot[patch]
        source = (slots // CAP).astype(jnp.int32)
        place = (slots % CAP).astype(jnp.int32)
        local = send_ids[source, patch, place]
        valid = (place < send_counts[source, patch]).astype(coarse.dtype)
        picked = coarse[(source * BLK_DEV + local).astype(jnp.int32)] * valid[:, None, None]
        weight_tables = interpolation_weights[entry_weight_pattern[patch]]
        picked = picked.reshape(NSUB, SUBTILE_ENTRIES, C0, BLK).astype(jnp.float32)
        weight_tables = weight_tables.reshape(NSUB, SUBTILE_ENTRIES, BLK, SUBPIX).astype(jnp.float32)
        blended = jnp.einsum("jecb,jebt->jct", picked, weight_tables, precision=lax.Precision.HIGHEST)
        blended = blended.astype(jnp.bfloat16).astype(jnp.float32)
        lifted_features = jnp.einsum("jct,cf->jtf", blended, lift_wide, precision=lax.Precision.HIGHEST)
        lifted_features = lifted_features.astype(jnp.bfloat16).reshape(PATCH_ROWS // SUBTILE_ROWS, PATCH_COLUMNS // SUBTILE_COLUMNS, SUBTILE_ROWS, SUBTILE_COLUMNS, FINE_CHANNELS)
        return lifted_features.transpose(0, 2, 1, 3, 4).reshape(PATCH_ROWS, PATCH_COLUMNS, FINE_CHANNELS)

    patches = lax.map(one_patch, jnp.arange(DEVICES, dtype=jnp.int32))
    guidance = patches.reshape(N_PY, N_PX, PATCH_ROWS, PATCH_COLUMNS, FINE_CHANNELS).transpose(0, 2, 1, 3, 4).reshape(GH, GW, FINE_CHANNELS)
    first = (features.astype(jnp.float32) + jax.nn.silu(conv_three(features, conv_a) + guidance.astype(jnp.float32))).astype(jnp.bfloat16)
    pooled = first.astype(jnp.float32).reshape(GH // 2, 2, GW // 2, 2, FINE_CHANNELS).mean(axis=(1, 3)).astype(jnp.bfloat16)
    second = jax.nn.silu(conv_three(pooled, conv_b)).astype(jnp.bfloat16)
    projected = jnp.dot(second, up_weight, preferred_element_type=jnp.float32)
    upsampled = jnp.repeat(jnp.repeat(projected, 2, axis=0), 2, axis=1)
    return (first.astype(jnp.float32) + upsampled).astype(jnp.bfloat16)
```

```python
import jax
import jax.numpy as jnp
from jax import lax
from jax.experimental import pallas as pl
from jax.experimental.pallas import tpu as pltpu
from jax.sharding import PartitionSpec as P

F32 = jnp.float32
BF16 = jnp.bfloat16
MIB = 1024 * 1024

SUBTILE_ENTRIES = 4
SUBTILE_ROWS = 8
SUBTILE_COLUMNS = 16
PY = 8
PX = 16
DEVICES = PY * PX
OWNED = 8
CELLS = 128
CHANNELS = 100
PART = 7
SLOT = 8
PATTERNS = 8
SUBTILES = 64
ENTRIES = SUBTILES * SUBTILE_ENTRIES
ROWS = 64
COLUMNS = 128
FINE = 256
WIDE = 512
TILES = DEVICES * OWNED
ZERO_TILE = PATTERNS * TILES


def silu(v):
    return 0.5 * v * (1.0 + jnp.tanh(0.5 * v))


def dot(a, b):
    return jnp.dot(a, b, preferred_element_type=F32)


def pack_kernel(coarse_ref, tables_ref, out_ref, parts_ref):
    @pl.when(pl.program_id(0) == 0)
    def _():
        row = lax.broadcasted_iota(jnp.int32, (PX * SLOT, CHANNELS), 0)
        channel = lax.broadcasted_iota(jnp.int32, (PX * SLOT, CHANNELS), 1)
        place = row % SLOT
        chosen = (channel == (row // SLOT) * PART + place) & (place < PART)
        pick = jnp.where(chosen, 1.0, 0.0).astype(BF16)
        for block in range(OWNED):
            parts_ref[:, block] = dot(pick, coarse_ref[block]).reshape(PX, SLOT, CELLS)

    place = lax.broadcasted_iota(jnp.int32, (PX, OWNED, SLOT, CELLS), 2)
    tables = jnp.broadcast_to(tables_ref[0][None, :, None, :], place.shape)
    merged = jnp.where(place == PART, tables, parts_ref[...])
    out_ref[0] = merged.reshape(PX, OWNED * SLOT, CELLS).astype(BF16)


def pack(coarse, tables):
    return pl.pallas_call(
        pack_kernel,
        grid=(PY,),
        in_specs=[
            pl.BlockSpec((OWNED, CHANNELS, CELLS), lambda i: (0, 0, 0)),
            pl.BlockSpec((1, OWNED, CELLS), lambda i: (i, 0, 0)),
        ],
        out_specs=pl.BlockSpec((1, PX, OWNED * SLOT, CELLS), lambda i: (i, 0, 0, 0)),
        out_shape=jax.ShapeDtypeStruct((PY, PX, OWNED * SLOT, CELLS), BF16),
        scratch_shapes=[pltpu.VMEM((PX, OWNED, SLOT, CELLS), F32)],
        compiler_params=pltpu.CompilerParams(vmem_limit_bytes=24 * MIB),
    )(coarse, tables)


def blend_kernel(index_ref, blocks_ref, weights_ref, out_ref, table_ref):
    chunk = 1024

    def multiply(step, carry):
        rows = pl.ds(pl.multiple_of(step * chunk, chunk), chunk)
        tiles = pl.ds(pl.multiple_of(step * (chunk // SLOT), chunk // SLOT), chunk // SLOT)
        part = blocks_ref[rows, :]
        for pair in range(PATTERNS // 2):
            both = jnp.concatenate([weights_ref[2 * pair], weights_ref[2 * pair + 1]], axis=1)
            product = dot(part, both)
            for half in range(2):
                table_ref[2 * pair + half, tiles] = product[:, half * CELLS : (half + 1) * CELLS].reshape(
                    chunk // SLOT, SLOT, CELLS
                )
        return carry

    lax.fori_loop(0, TILES * SLOT // chunk, multiply, 0)
    table_ref[PATTERNS, 0] = jnp.zeros((SLOT, CELLS), F32)

    def total(base):
        tile = [table_ref[index_ref[base + i] // TILES, index_ref[base + i] % TILES] for i in range(SUBTILE_ENTRIES)]
        return (tile[0] + tile[1]) + (tile[2] + tile[3])

    group = 8

    def gather(step, carry):
        base = step * (group * SUBTILE_ENTRIES)
        sums = [total(base + k * SUBTILE_ENTRIES) for k in range(group)]
        rows = pl.ds(pl.multiple_of(step * group * SLOT, group * SLOT), group * SLOT)
        out_ref[rows, :] = jnp.concatenate(sums, axis=0).astype(BF16)
        return carry

    lax.fori_loop(0, PX * SUBTILES // group, gather, 0)


def blend(index, blocks, weights):
    return pl.pallas_call(
        blend_kernel,
        in_specs=[
            pl.BlockSpec(memory_space=pltpu.SMEM),
            pl.BlockSpec(memory_space=pltpu.VMEM),
            pl.BlockSpec(memory_space=pltpu.VMEM),
        ],
        out_specs=pl.BlockSpec(memory_space=pltpu.VMEM),
        out_shape=jax.ShapeDtypeStruct((PX * SUBTILES * SLOT, CELLS), BF16),
        scratch_shapes=[pltpu.VMEM((PATTERNS + 1, TILES, SLOT, CELLS), F32)],
        compiler_params=pltpu.CompilerParams(vmem_limit_bytes=56 * MIB),
    )(index, blocks, weights)


def entry_index(received):
    rows = received.reshape(DEVICES, OWNED, SLOT, CELLS)[:, :, PART, :]
    sent = rows[:, 4, : 3 * PX].astype(jnp.int32)
    owner = lax.broadcasted_iota(jnp.int32, (PX, DEVICES), 1)
    counts = sent[:, 2 * PX : 3 * PX].T
    where = [
        jnp.where(k < counts, owner * OWNED + sent[:, k * PX : (k + 1) * PX].T, -1) for k in range(2)
    ]
    mine = lax.dynamic_slice_in_dim(rows, lax.axis_index("py") * PX, PX, axis=0).astype(jnp.int32)
    slot = mine[:, 0:2].reshape(PX, ENTRIES)
    pattern = mine[:, 2:4].reshape(PX, ENTRIES)
    owner_at = lax.broadcasted_iota(jnp.int32, (PX, ENTRIES, DEVICES), 2)
    found = jnp.where(slot[:, :, None] % 2 == 0, where[0][:, None, :], where[1][:, None, :])
    block = jnp.sum(jnp.where(slot[:, :, None] // 2 == owner_at, found, 0), axis=2)
    return jnp.where(block >= 0, pattern * TILES + block, ZERO_TILE).reshape(PX * ENTRIES)


def shifted(rows, left, right):
    wide = rows.astype(F32)
    column = lax.broadcasted_iota(jnp.int32, wide.shape, 0)
    last = wide.shape[0] - 1
    before = jnp.where(column == 0, jnp.broadcast_to(left, wide.shape), pltpu.roll(wide, 1, 0))
    after = jnp.where(column == last, jnp.broadcast_to(right, wide.shape), pltpu.roll(wide, last, 0))
    return before.astype(BF16), rows, after.astype(BF16)


def fill(taps_ref, row, cells, left_ref, right_ref):
    depth = cells.shape[-1]
    parts = shifted(cells, left_ref[row], right_ref[row])
    for k in range(3):
        taps_ref[row, :, k * depth : (k + 1) * depth] = parts[k]


def fill_all(taps_ref, cells_ref, top_ref, bottom_ref, left_ref, right_ref):
    count = cells_ref.shape[0]
    fill(taps_ref, 0, top_ref[0], left_ref, right_ref)

    def one(row, carry):
        fill(taps_ref, row + 1, cells_ref[row], left_ref, right_ref)
        return carry

    lax.fori_loop(0, count, one, 0)
    fill(taps_ref, count + 1, bottom_ref[0], left_ref, right_ref)


def taps_dot(taps_ref, weights_ref, first_row, count):
    columns, depth = taps_ref.shape[1], taps_ref.shape[2]
    total = None
    for row_off in range(3):
        rows = taps_ref[pl.ds(first_row + row_off, count)].reshape(count * columns, depth)
        product = dot(rows, weights_ref[row_off])
        total = product if total is None else total + product
    return total


STRIP = 8


def conv_kernel(cells_ref, top_ref, bottom_ref, left_ref, right_ref, weights_ref, out_ref, taps_ref):
    step = pl.program_id(0)

    @pl.when(step == 0)
    def _():
        fill_all(taps_ref, cells_ref, top_ref, bottom_ref, left_ref, right_ref)

    out_ref[...] = taps_dot(taps_ref, weights_ref, step * STRIP, STRIP).reshape(STRIP, COLUMNS, FINE)


def whole(*shape):
    return pl.BlockSpec(shape, lambda i: (0,) * len(shape))


def conv_fine(cells, halo, weights):
    return pl.pallas_call(
        conv_kernel,
        grid=(ROWS // STRIP,),
        in_specs=[
            whole(ROWS, COLUMNS, FINE),
            whole(1, COLUMNS, FINE),
            whole(1, COLUMNS, FINE),
            whole(ROWS + 2, 1, FINE),
            whole(ROWS + 2, 1, FINE),
            whole(3, 3 * FINE, FINE),
        ],
        out_specs=pl.BlockSpec((STRIP, COLUMNS, FINE), lambda i: (i, 0, 0)),
        out_shape=jax.ShapeDtypeStruct((ROWS, COLUMNS, FINE), F32),
        scratch_shapes=[pltpu.VMEM((ROWS + 2, COLUMNS, 3 * FINE), BF16)],
        compiler_params=pltpu.CompilerParams(vmem_limit_bytes=48 * MIB),
    )(cells, *halo, weights)


def first_kernel(blended_ref, lift_ref, conv_ref, cells_ref, first_ref, pooled_ref):
    cell = lax.broadcasted_iota(jnp.int32, (32, CELLS), 1)
    target = lax.broadcasted_iota(jnp.int32, (32, CELLS), 0)
    row = cell // SUBTILE_COLUMNS
    column = cell % SUBTILE_COLUMNS
    pool = jnp.where((row // 2) * 8 + column // 2 == target, 0.25, 0.0).astype(BF16)
    for pair in range(COLUMNS // SUBTILE_COLUMNS // 2):
        both = blended_ref[:, pair * 2 * SLOT : (pair + 1) * 2 * SLOT, :].astype(F32)
        for half in range(2):
            tile = 2 * pair + half
            columns = slice(tile * SUBTILE_COLUMNS, (tile + 1) * SUBTILE_COLUMNS)
            part = both[:, half * SLOT : (half + 1) * SLOT, :].reshape(PX * SLOT, CELLS).astype(BF16)
            guidance = lax.dot_general(
                part, lift_ref[...], (((0,), (0,)), ((), ())), preferred_element_type=F32
            ).astype(BF16)
            summed = conv_ref[:, columns, :].reshape(CELLS, FINE) + guidance.astype(F32)
            kept = cells_ref[:, columns, :].reshape(CELLS, FINE).astype(F32)
            first = (kept + silu(summed)).astype(BF16)
            first_ref[:, columns, :] = first.reshape(SUBTILE_ROWS, SUBTILE_COLUMNS, FINE)
            pooled_ref[:, tile * 8 : (tile + 1) * 8, :] = dot(pool, first).reshape(4, 8, FINE).astype(BF16)


def first_level(blended, lift, conv, cells):
    strip = pl.BlockSpec((STRIP, COLUMNS, FINE), lambda i: (i, 0, 0))
    return pl.pallas_call(
        first_kernel,
        grid=(ROWS // STRIP,),
        in_specs=[
            pl.BlockSpec((PX, 8 * SLOT, CELLS), lambda i: (0, i, 0)),
            whole(PX * SLOT, FINE),
            strip,
            strip,
        ],
        out_specs=[strip, pl.BlockSpec((STRIP // 2, COLUMNS // 2, FINE), lambda i: (i, 0, 0))],
        out_shape=[
            jax.ShapeDtypeStruct((ROWS, COLUMNS, FINE), BF16),
            jax.ShapeDtypeStruct((ROWS // 2, COLUMNS // 2, FINE), BF16),
        ],
        compiler_params=pltpu.CompilerParams(vmem_limit_bytes=32 * MIB),
    )(blended, lift, conv, cells)


SECOND = 8


def second_kernel(
    pooled_ref, top_ref, bottom_ref, left_ref, right_ref, weights_ref, up_ref, first_ref, out_ref, taps_ref, spread_ref
):
    step = pl.program_id(0)

    @pl.when(step == 0)
    def _():
        fill_all(taps_ref, pooled_ref, top_ref, bottom_ref, left_ref, right_ref)

    second = silu(taps_dot(taps_ref, weights_ref, step * SECOND, SECOND)).astype(BF16)
    projected = dot(second, up_ref[...])
    half = COLUMNS // 2
    for lane in range(FINE // 128):
        part = projected[:, lane * 128 : (lane + 1) * 128]
        for side in range(2):
            spread_ref[lane, pl.ds(side, SECOND * half, stride=2), :] = part
    for lane in range(FINE // 128):
        lanes = slice(lane * 128, (lane + 1) * 128)
        for row in range(SECOND):
            added = spread_ref[lane, row * COLUMNS : (row + 1) * COLUMNS, :]
            for side in range(2):
                first = first_ref[2 * row + side, :, lanes].astype(F32)
                out_ref[2 * row + side, :, lanes] = (first + added).astype(BF16)


def second_level(pooled, halo, weights, up, first):
    strip = pl.BlockSpec((2 * SECOND, COLUMNS, FINE), lambda i: (i, 0, 0))
    return pl.pallas_call(
        second_kernel,
        grid=(ROWS // 2 // SECOND,),
        in_specs=[
            whole(ROWS // 2, COLUMNS // 2, FINE),
            whole(1, COLUMNS // 2, FINE),
            whole(1, COLUMNS // 2, FINE),
            whole(ROWS // 2 + 2, 1, FINE),
            whole(ROWS // 2 + 2, 1, FINE),
            whole(3, 3 * FINE, WIDE),
            whole(WIDE, FINE),
            strip,
        ],
        out_specs=strip,
        out_shape=jax.ShapeDtypeStruct((ROWS, COLUMNS, FINE), BF16),
        scratch_shapes=[
            pltpu.VMEM((ROWS // 2 + 2, COLUMNS // 2, 3 * FINE), BF16),
            pltpu.VMEM((FINE // 128, SECOND * COLUMNS, 128), F32),
        ],
        compiler_params=pltpu.CompilerParams(vmem_limit_bytes=48 * MIB),
    )(pooled, *halo, weights, up, first)


def halo_of(cells):
    down = [(i, i + 1) for i in range(PY - 1)]
    up = [(i + 1, i) for i in range(PY - 1)]
    top = lax.ppermute(cells[-1:], "py", down)
    bottom = lax.ppermute(cells[:1], "py", up)

    def column(at):
        return jnp.concatenate([top[:, at], cells[:, at], bottom[:, at]], axis=0)

    left = lax.ppermute(column(-1), "px", [(i, i + 1) for i in range(PX - 1)])
    right = lax.ppermute(column(0), "px", [(i + 1, i) for i in range(PX - 1)])
    return top, bottom, left[:, None].astype(F32), right[:, None].astype(F32)


def local(
    features,
    coarse,
    send_ids,
    send_counts,
    entry_slot,
    entry_weight_pattern,
    interpolation_weights,
    lift_weight,
    conv_a,
    conv_b,
    up_weight,
):
    ids = send_ids[0].reshape(PY, PX, 2)
    sent = jnp.concatenate([ids[:, :, 0], ids[:, :, 1], send_counts[0].reshape(PY, PX)], axis=1)
    sent = jnp.pad(sent, ((0, 0), (0, CELLS - 3 * PX)))[:, None]
    named = jnp.concatenate([entry_slot[0].reshape(2, CELLS), entry_weight_pattern[0].reshape(2, CELLS)], axis=0)
    named = jnp.broadcast_to(named[None], (PY, 4, CELLS))
    tables = jnp.concatenate([named, sent, jnp.zeros((PY, 3, CELLS), jnp.int32)], axis=1).astype(F32)
    outgoing = pack(coarse, tables).reshape(DEVICES, OWNED * SLOT, CELLS)
    received = lax.all_to_all(outgoing, ("py", "px"), split_axis=0, concat_axis=0, tiled=True)
    index = entry_index(received)
    parts = blend(index, received.reshape(TILES * SLOT, CELLS), interpolation_weights)
    blended = lax.all_to_all(
        parts.reshape(PX, SUBTILES * SLOT, CELLS), "px", split_axis=0, concat_axis=0, tiled=True
    )
    conv = conv_fine(features, halo_of(features), conv_a.reshape(3, 3 * FINE, FINE))
    lift = jnp.pad(lift_weight, ((0, PX * PART - CHANNELS), (0, 0))).reshape(PX, PART, FINE)
    lift = jnp.pad(lift, ((0, 0), (0, SLOT - PART), (0, 0))).reshape(PX * SLOT, FINE)
    first, pooled = first_level(blended, lift, conv, features)
    return second_level(pooled, halo_of(pooled), conv_b.reshape(3, 3 * FINE, WIDE), up_weight, first)


def solution(mesh):
    placed = (
        P("py", "px", None),
        P(("py", "px"), None, None),
        P(("py", "px"), None, None),
        P(("py", "px"), None),
        P(("py", "px"), None),
        P(("py", "px"), None),
        P(),
        P(),
        P(),
        P(),
        P(),
    )
    return jax.shard_map(
        local, mesh=mesh, in_specs=placed, out_specs=P("py", "px", None), check_vma=False
    )
```

```python
import jax
import jax.numpy as jnp
from jax import lax
from jax.experimental import pallas as pl
from jax.experimental.pallas import tpu as pltpu
from jax.sharding import Mesh
from jax.sharding import PartitionSpec as P

F32 = jnp.float32
BF16 = jnp.bfloat16
MIB = 1024 * 1024

SUBTILE_ENTRIES = 4
SUBTILE_ROWS = 8
SUBTILE_COLUMNS = 16
Z = 4
CORES = 2
PY = Z * CORES
PX = 16
NEAR = PY // CORES * PX
DEVICES = PY * PX
OWNED = 8
CELLS = 128
CHANNELS = 100
PART = 7
SLOT = 8
PATTERNS = 8
SUBTILES = 64
ENTRIES = SUBTILES * SUBTILE_ENTRIES
ROWS = 64
COLUMNS = 128
FINE = 256
WIDE = 512
TILES = DEVICES * OWNED
ZERO_TILE = PATTERNS * TILES


def silu(v):
    return 0.5 * v * (1.0 + jnp.tanh(0.5 * v))


def dot(a, b):
    return jnp.dot(a, b, preferred_element_type=F32)


def pack_kernel(coarse_ref, tables_ref, out_ref, parts_ref):
    @pl.when(pl.program_id(0) == 0)
    def _():
        row = lax.broadcasted_iota(jnp.int32, (PX * SLOT, CHANNELS), 0)
        channel = lax.broadcasted_iota(jnp.int32, (PX * SLOT, CHANNELS), 1)
        place = row % SLOT
        chosen = (channel == (row // SLOT) * PART + place) & (place < PART)
        pick = jnp.where(chosen, 1.0, 0.0).astype(BF16)
        for block in range(OWNED):
            parts_ref[:, block] = dot(pick, coarse_ref[block]).reshape(PX, SLOT, CELLS)

    place = lax.broadcasted_iota(jnp.int32, (PX, OWNED, SLOT, CELLS), 2)
    tables = jnp.broadcast_to(tables_ref[0][None, :, None, :], place.shape)
    merged = jnp.where(place == PART, tables, parts_ref[...])
    out_ref[0] = merged.reshape(PX, OWNED * SLOT, CELLS).astype(BF16)


def pack(coarse, tables):
    return pl.pallas_call(
        pack_kernel,
        grid=(Z,),
        in_specs=[
            pl.BlockSpec((OWNED, CHANNELS, CELLS), lambda i: (0, 0, 0)),
            pl.BlockSpec((1, OWNED, CELLS), lambda i: (i, 0, 0)),
        ],
        out_specs=pl.BlockSpec((1, PX, OWNED * SLOT, CELLS), lambda i: (i, 0, 0, 0)),
        out_shape=jax.ShapeDtypeStruct((Z, PX, OWNED * SLOT, CELLS), BF16),
        scratch_shapes=[pltpu.VMEM((PX, OWNED, SLOT, CELLS), F32)],
        compiler_params=pltpu.CompilerParams(vmem_limit_bytes=24 * MIB),
    )(coarse, tables)


def blend_kernel(index_ref, own_ref, other_ref, weights_ref, out_ref, table_ref):
    chunk = 1024

    def multiply(blocks_ref, first, step):
        rows = pl.ds(pl.multiple_of(step * chunk, chunk), chunk)
        part = blocks_ref[rows, :]
        for pair in range(PATTERNS // 2):
            both = jnp.concatenate([weights_ref[2 * pair], weights_ref[2 * pair + 1]], axis=1)
            product = dot(part, both)
            for half in range(2):
                tiles = pl.ds((2 * pair + half) * TILES + first + step * (chunk // SLOT), chunk // SLOT)
                lanes = slice(half * CELLS, (half + 1) * CELLS)
                table_ref[tiles] = product[:, lanes].reshape(chunk // SLOT, SLOT, CELLS)

    for first, blocks_ref in ((0, own_ref), (TILES // 2, other_ref)):

        def one(step, carry):
            multiply(blocks_ref, first, step)
            return carry

        lax.fori_loop(0, TILES // 2 * SLOT // chunk, one, 0)
    table_ref[ZERO_TILE] = jnp.zeros((SLOT, CELLS), F32)

    def total(base):
        tile = [table_ref[index_ref[base + i]] for i in range(SUBTILE_ENTRIES)]
        return (tile[0] + tile[1]) + (tile[2] + tile[3])

    group = 32

    def gather(step, carry):
        base = step * (group * SUBTILE_ENTRIES)
        sums = [total(base + k * SUBTILE_ENTRIES) for k in range(group)]
        for k in range(0, group, 2):
            rows = pl.ds(pl.multiple_of((step * group + k) * SLOT, 2 * SLOT), 2 * SLOT)
            out_ref[rows, :] = jnp.concatenate(sums[k : k + 2], axis=0).astype(BF16)
        return carry

    lax.fori_loop(0, PX * SUBTILES // group, gather, 0)


def blend(index, own, other, weights):
    return pl.pallas_call(
        blend_kernel,
        in_specs=[
            pl.BlockSpec(memory_space=pltpu.SMEM),
            pl.BlockSpec(memory_space=pltpu.VMEM),
            pl.BlockSpec(memory_space=pltpu.VMEM),
            pl.BlockSpec(memory_space=pltpu.VMEM),
        ],
        out_specs=pl.BlockSpec(memory_space=pltpu.VMEM),
        out_shape=jax.ShapeDtypeStruct((PX * SUBTILES * SLOT, CELLS), BF16),
        scratch_shapes=[pltpu.VMEM((ZERO_TILE + 1, SLOT, CELLS), F32)],
        compiler_params=pltpu.CompilerParams(vmem_limit_bytes=42 * MIB),
    )(index, own, other, weights)


def entry_index(own, other):
    core = lax.axis_index("core")

    def tables(part):
        return part.reshape(NEAR, OWNED, SLOT, CELLS)[:, :, PART, :]

    rows = jnp.concatenate([tables(own), tables(other)], axis=0)
    mine = lax.dynamic_slice_in_dim(rows[:NEAR], lax.axis_index("z") * PX, PX, axis=0).astype(jnp.int32)
    slot = mine[:, 0:2].reshape(PX, ENTRIES)
    pattern = mine[:, 2:4].reshape(PX, ENTRIES)
    sent = lax.dynamic_slice_in_dim(rows[:, 4], core * 3 * PX, 3 * PX, axis=1).astype(jnp.int32)
    sender = lax.broadcasted_iota(jnp.int32, (PX, DEVICES), 1)
    counts = sent[:, 2 * PX : 3 * PX].T
    where = [
        jnp.where(k < counts, sender * OWNED + sent[:, k * PX : (k + 1) * PX].T, -1) for k in range(2)
    ]
    owner = slot // 2
    near = owner // (CORES * PX) * PX + owner % PX
    place = near + jnp.where(owner // PX % CORES == core, 0, NEAR)
    sender_at = lax.broadcasted_iota(jnp.int32, (PX, ENTRIES, DEVICES), 2)
    found = jnp.where(slot[:, :, None] % 2 == 0, where[0][:, None, :], where[1][:, None, :])
    block = jnp.sum(jnp.where(place[:, :, None] == sender_at, found, 0), axis=2)
    return jnp.where(block >= 0, pattern * TILES + block, ZERO_TILE).reshape(PX * ENTRIES)


def shifted(rows, left, right):
    wide = rows.astype(F32)
    column = lax.broadcasted_iota(jnp.int32, wide.shape, 0)
    last = wide.shape[0] - 1
    before = jnp.where(column == 0, jnp.broadcast_to(left, wide.shape), pltpu.roll(wide, 1, 0))
    after = jnp.where(column == last, jnp.broadcast_to(right, wide.shape), pltpu.roll(wide, last, 0))
    return before.astype(BF16), rows, after.astype(BF16)


def fill(taps_ref, row, cells, left_ref, right_ref):
    depth = cells.shape[-1]
    parts = shifted(cells, left_ref[row], right_ref[row])
    for k in range(3):
        taps_ref[row, :, k * depth : (k + 1) * depth] = parts[k]


def fill_all(taps_ref, cells_ref, top_ref, bottom_ref, left_ref, right_ref):
    count = cells_ref.shape[0]
    fill(taps_ref, 0, top_ref[0], left_ref, right_ref)

    def one(row, carry):
        fill(taps_ref, row + 1, cells_ref[row], left_ref, right_ref)
        return carry

    lax.fori_loop(0, count, one, 0)
    fill(taps_ref, count + 1, bottom_ref[0], left_ref, right_ref)


def taps_dot(taps_ref, weights_ref, first_row, count):
    columns, depth = taps_ref.shape[1], taps_ref.shape[2]
    total = None
    for row_off in range(3):
        rows = taps_ref[pl.ds(first_row + row_off, count)].reshape(count * columns, depth)
        product = dot(rows, weights_ref[row_off])
        total = product if total is None else total + product
    return total


STRIP = 8


def conv_kernel(cells_ref, top_ref, bottom_ref, left_ref, right_ref, weights_ref, out_ref, taps_ref):
    step = pl.program_id(0)

    @pl.when(step == 0)
    def _():
        fill_all(taps_ref, cells_ref, top_ref, bottom_ref, left_ref, right_ref)

    out_ref[...] = taps_dot(taps_ref, weights_ref, step * STRIP, STRIP).reshape(STRIP, COLUMNS, FINE)


def whole(*shape):
    return pl.BlockSpec(shape, lambda i: (0,) * len(shape))


def conv_fine(cells, halo, weights):
    return pl.pallas_call(
        conv_kernel,
        grid=(ROWS // STRIP,),
        in_specs=[
            whole(ROWS, COLUMNS, FINE),
            whole(1, COLUMNS, FINE),
            whole(1, COLUMNS, FINE),
            whole(ROWS + 2, 1, FINE),
            whole(ROWS + 2, 1, FINE),
            whole(3, 3 * FINE, FINE),
        ],
        out_specs=pl.BlockSpec((STRIP, COLUMNS, FINE), lambda i: (i, 0, 0)),
        out_shape=jax.ShapeDtypeStruct((ROWS, COLUMNS, FINE), F32),
        scratch_shapes=[pltpu.VMEM((ROWS + 2, COLUMNS, 3 * FINE), BF16)],
        compiler_params=pltpu.CompilerParams(vmem_limit_bytes=48 * MIB),
    )(cells, *halo, weights)


def first_kernel(blended_ref, lift_ref, conv_ref, cells_ref, first_ref, pooled_ref):
    cell = lax.broadcasted_iota(jnp.int32, (32, CELLS), 1)
    target = lax.broadcasted_iota(jnp.int32, (32, CELLS), 0)
    row = cell // SUBTILE_COLUMNS
    column = cell % SUBTILE_COLUMNS
    pool = jnp.where((row // 2) * 8 + column // 2 == target, 0.25, 0.0).astype(BF16)
    for pair in range(COLUMNS // SUBTILE_COLUMNS // 2):
        both = blended_ref[:, pair * 2 * SLOT : (pair + 1) * 2 * SLOT, :].astype(F32)
        for half in range(2):
            tile = 2 * pair + half
            columns = slice(tile * SUBTILE_COLUMNS, (tile + 1) * SUBTILE_COLUMNS)
            part = both[:, half * SLOT : (half + 1) * SLOT, :].reshape(PX * SLOT, CELLS).astype(BF16)
            guidance = lax.dot_general(
                part, lift_ref[...], (((0,), (0,)), ((), ())), preferred_element_type=F32
            ).astype(BF16)
            summed = conv_ref[:, columns, :].reshape(CELLS, FINE) + guidance.astype(F32)
            kept = cells_ref[:, columns, :].reshape(CELLS, FINE).astype(F32)
            first = (kept + silu(summed)).astype(BF16)
            first_ref[:, columns, :] = first.reshape(SUBTILE_ROWS, SUBTILE_COLUMNS, FINE)
            pooled_ref[:, tile * 8 : (tile + 1) * 8, :] = dot(pool, first).reshape(4, 8, FINE).astype(BF16)


def first_level(blended, lift, conv, cells):
    strip = pl.BlockSpec((STRIP, COLUMNS, FINE), lambda i: (i, 0, 0))
    return pl.pallas_call(
        first_kernel,
        grid=(ROWS // STRIP,),
        in_specs=[
            pl.BlockSpec((PX, 8 * SLOT, CELLS), lambda i: (0, i, 0)),
            whole(PX * SLOT, FINE),
            strip,
            strip,
        ],
        out_specs=[strip, pl.BlockSpec((STRIP // 2, COLUMNS // 2, FINE), lambda i: (i, 0, 0))],
        out_shape=[
            jax.ShapeDtypeStruct((ROWS, COLUMNS, FINE), BF16),
            jax.ShapeDtypeStruct((ROWS // 2, COLUMNS // 2, FINE), BF16),
        ],
        compiler_params=pltpu.CompilerParams(vmem_limit_bytes=32 * MIB),
    )(blended, lift, conv, cells)


SECOND = 8


def second_kernel(
    pooled_ref, top_ref, bottom_ref, left_ref, right_ref, weights_ref, up_ref, first_ref, out_ref, taps_ref, spread_ref
):
    step = pl.program_id(0)

    @pl.when(step == 0)
    def _():
        fill_all(taps_ref, pooled_ref, top_ref, bottom_ref, left_ref, right_ref)

    second = silu(taps_dot(taps_ref, weights_ref, step * SECOND, SECOND)).astype(BF16)
    projected = dot(second, up_ref[...])
    half = COLUMNS // 2
    for lane in range(FINE // 128):
        part = projected[:, lane * 128 : (lane + 1) * 128]
        for side in range(2):
            spread_ref[lane, pl.ds(side, SECOND * half, stride=2), :] = part
    for lane in range(FINE // 128):
        lanes = slice(lane * 128, (lane + 1) * 128)
        for row in range(SECOND):
            added = spread_ref[lane, row * COLUMNS : (row + 1) * COLUMNS, :]
            for side in range(2):
                first = first_ref[2 * row + side, :, lanes].astype(F32)
                out_ref[2 * row + side, :, lanes] = (first + added).astype(BF16)


def second_level(pooled, halo, weights, up, first):
    strip = pl.BlockSpec((2 * SECOND, COLUMNS, FINE), lambda i: (i, 0, 0))
    return pl.pallas_call(
        second_kernel,
        grid=(ROWS // 2 // SECOND,),
        in_specs=[
            whole(ROWS // 2, COLUMNS // 2, FINE),
            whole(1, COLUMNS // 2, FINE),
            whole(1, COLUMNS // 2, FINE),
            whole(ROWS // 2 + 2, 1, FINE),
            whole(ROWS // 2 + 2, 1, FINE),
            whole(3, 3 * FINE, WIDE),
            whole(WIDE, FINE),
            strip,
        ],
        out_specs=strip,
        out_shape=jax.ShapeDtypeStruct((ROWS, COLUMNS, FINE), BF16),
        scratch_shapes=[
            pltpu.VMEM((ROWS // 2 + 2, COLUMNS // 2, 3 * FINE), BF16),
            pltpu.VMEM((FINE // 128, SECOND * COLUMNS, 128), F32),
        ],
        compiler_params=pltpu.CompilerParams(vmem_limit_bytes=48 * MIB),
    )(pooled, *halo, weights, up, first)


ROWS_AXES = ("z", "core")


def halo_of(cells):
    down = [(i, i + 1) for i in range(PY - 1)]
    up = [(i + 1, i) for i in range(PY - 1)]
    top = lax.ppermute(cells[-1:], ROWS_AXES, down)
    bottom = lax.ppermute(cells[:1], ROWS_AXES, up)

    def column(at):
        return jnp.concatenate([top[:, at], cells[:, at], bottom[:, at]], axis=0)

    left = lax.ppermute(column(-1), "px", [(i, i + 1) for i in range(PX - 1)])
    right = lax.ppermute(column(0), "px", [(i + 1, i) for i in range(PX - 1)])
    return top, bottom, left[:, None].astype(F32), right[:, None].astype(F32)


def local(
    features,
    coarse,
    send_ids,
    send_counts,
    entry_slot,
    entry_weight_pattern,
    interpolation_weights,
    lift_weight,
    conv_a,
    conv_b,
    up_weight,
):
    edges = halo_of(features)
    ids = send_ids[0].reshape(Z, CORES, PX, 2).transpose(0, 1, 3, 2).reshape(Z, CORES, 2 * PX)
    sent = jnp.concatenate([ids, send_counts[0].reshape(Z, CORES, PX)], axis=2).reshape(Z, 1, CORES * 3 * PX)
    sent = jnp.pad(sent, ((0, 0), (0, 0), (0, CELLS - CORES * 3 * PX)))
    named = jnp.concatenate([entry_slot[0].reshape(2, CELLS), entry_weight_pattern[0].reshape(2, CELLS)], axis=0)
    named = jnp.broadcast_to(named[None], (Z, 4, CELLS))
    tables = jnp.concatenate([named, sent, jnp.zeros((Z, 3, CELLS), jnp.int32)], axis=1).astype(F32)
    outgoing = pack(coarse, tables).reshape(NEAR, OWNED * SLOT, CELLS)
    own = lax.all_to_all(outgoing, ("z", "px"), split_axis=0, concat_axis=0, tiled=True)
    other = lax.ppermute(own, "core", [(0, 1), (1, 0)])
    index = entry_index(own, other)
    index, edges = lax.optimization_barrier((index, edges))
    half = (NEAR * OWNED * SLOT, CELLS)
    parts = blend(index, own.reshape(half), other.reshape(half), interpolation_weights)
    blended = lax.all_to_all(
        parts.reshape(PX, SUBTILES * SLOT, CELLS), "px", split_axis=0, concat_axis=0, tiled=True
    )
    conv = conv_fine(features, edges, conv_a.reshape(3, 3 * FINE, FINE))
    lift = jnp.pad(lift_weight, ((0, PX * PART - CHANNELS), (0, 0))).reshape(PX, PART, FINE)
    lift = jnp.pad(lift, ((0, 0), (0, SLOT - PART), (0, 0))).reshape(PX * SLOT, FINE)
    first, pooled = first_level(blended, lift, conv, features)
    return second_level(pooled, halo_of(pooled), conv_b.reshape(3, 3 * FINE, WIDE), up_weight, first)


def solution(mesh):
    split = Mesh(mesh.devices.reshape(Z, CORES, PX), ("z", "core", "px"))
    every = ("z", "core", "px")
    placed = (
        P(ROWS_AXES, "px", None),
        P(every, None, None),
        P(every, None, None),
        P(every, None),
        P(every, None),
        P(every, None),
        P(),
        P(),
        P(),
        P(),
        P(),
    )
    return jax.shard_map(
        local, mesh=split, in_specs=placed, out_specs=P(ROWS_AXES, "px", None), check_vma=False
    )
```

```python
import jax
import jax.numpy as jnp
from jax import lax
from jax.experimental import pallas as pl
from jax.experimental.pallas import tpu as pltpu
from jax.sharding import Mesh
from jax.sharding import PartitionSpec as P

F32 = jnp.float32
BF16 = jnp.bfloat16
MIB = 1024 * 1024

SUBTILE_ENTRIES = 4
SUBTILE_ROWS = 8
SUBTILE_COLUMNS = 16
Z = 4
CORES = 2
PY = Z * CORES
PX = 16
NEAR = PY // CORES * PX
DEVICES = PY * PX
OWNED = 8
CELLS = 128
CHANNELS = 100
PART = 7
SLOT = 8
PATTERNS = 8
SUBTILES = 64
ENTRIES = SUBTILES * SUBTILE_ENTRIES
ROWS = 64
COLUMNS = 128
FINE = 256
WIDE = 512
TILES = DEVICES * OWNED
ZERO_TILE = PATTERNS * TILES


def silu(v):
    return 0.5 * v * (1.0 + jnp.tanh(0.5 * v))


def dot(a, b):
    return jnp.dot(a, b, preferred_element_type=F32)


def pack_kernel(coarse_ref, tables_ref, out_ref, parts_ref):
    @pl.when(pl.program_id(0) == 0)
    def _():
        row = lax.broadcasted_iota(jnp.int32, (PX * SLOT, CHANNELS), 0)
        channel = lax.broadcasted_iota(jnp.int32, (PX * SLOT, CHANNELS), 1)
        place = row % SLOT
        chosen = (channel == (row // SLOT) * PART + place) & (place < PART)
        pick = jnp.where(chosen, 1.0, 0.0).astype(BF16)
        for block in range(OWNED):
            parts_ref[:, block] = dot(pick, coarse_ref[block]).reshape(PX, SLOT, CELLS)

    place = lax.broadcasted_iota(jnp.int32, (PX, OWNED, SLOT, CELLS), 2)
    tables = jnp.broadcast_to(tables_ref[0][None, :, None, :], place.shape)
    merged = jnp.where(place == PART, tables, parts_ref[...])
    out_ref[0] = merged.reshape(PX, OWNED * SLOT, CELLS).astype(BF16)


def pack(coarse, tables):
    return pl.pallas_call(
        pack_kernel,
        grid=(Z,),
        in_specs=[
            pl.BlockSpec((OWNED, CHANNELS, CELLS), lambda i: (0, 0, 0)),
            pl.BlockSpec((1, OWNED, CELLS), lambda i: (i, 0, 0)),
        ],
        out_specs=pl.BlockSpec((1, PX, OWNED * SLOT, CELLS), lambda i: (i, 0, 0, 0)),
        out_shape=jax.ShapeDtypeStruct((Z, PX, OWNED * SLOT, CELLS), BF16),
        scratch_shapes=[pltpu.VMEM((PX, OWNED, SLOT, CELLS), F32)],
        compiler_params=pltpu.CompilerParams(vmem_limit_bytes=24 * MIB),
    )(coarse, tables)


def blend_kernel(index_ref, own_ref, other_ref, weights_ref, out_ref, table_ref):
    chunk = 1024

    def multiply(blocks_ref, first, step):
        rows = pl.ds(pl.multiple_of(step * chunk, chunk), chunk)
        part = blocks_ref[rows, :]
        for pair in range(PATTERNS // 2):
            both = jnp.concatenate([weights_ref[2 * pair], weights_ref[2 * pair + 1]], axis=1)
            product = dot(part, both)
            for half in range(2):
                tiles = pl.ds((2 * pair + half) * TILES + first + step * (chunk // SLOT), chunk // SLOT)
                lanes = slice(half * CELLS, (half + 1) * CELLS)
                table_ref[tiles] = product[:, lanes].reshape(chunk // SLOT, SLOT, CELLS)

    for first, blocks_ref in ((0, own_ref), (TILES // 2, other_ref)):

        def one(step, carry):
            multiply(blocks_ref, first, step)
            return carry

        lax.fori_loop(0, TILES // 2 * SLOT // chunk, one, 0)
    table_ref[ZERO_TILE] = jnp.zeros((SLOT, CELLS), F32)

    def total(base):
        tile = [table_ref[index_ref[base + i]] for i in range(SUBTILE_ENTRIES)]
        return (tile[0] + tile[1]) + (tile[2] + tile[3])

    group = 32

    def gather(step, carry):
        base = step * (group * SUBTILE_ENTRIES)
        sums = [total(base + k * SUBTILE_ENTRIES) for k in range(group)]
        for k in range(0, group, 2):
            rows = pl.ds(pl.multiple_of((step * group + k) * SLOT, 2 * SLOT), 2 * SLOT)
            out_ref[rows, :] = jnp.concatenate(sums[k : k + 2], axis=0).astype(BF16)
        return carry

    lax.fori_loop(0, PX * SUBTILES // group, gather, 0)


def blend(index, own, other, weights):
    return pl.pallas_call(
        blend_kernel,
        in_specs=[
            pl.BlockSpec(memory_space=pltpu.SMEM),
            pl.BlockSpec(memory_space=pltpu.VMEM),
            pl.BlockSpec(memory_space=pltpu.VMEM),
            pl.BlockSpec(memory_space=pltpu.VMEM),
        ],
        out_specs=pl.BlockSpec(memory_space=pltpu.VMEM),
        out_shape=pltpu.HBM((PX * SUBTILES * SLOT, CELLS), BF16),
        scratch_shapes=[pltpu.VMEM((ZERO_TILE + 1, SLOT, CELLS), F32)],
        compiler_params=pltpu.CompilerParams(vmem_limit_bytes=42 * MIB),
    )(index, own, other, weights)


def entry_index(own, other):
    core = lax.axis_index("core")

    def tables(part):
        return part.reshape(NEAR, OWNED, SLOT, CELLS)[:, :, PART, :]

    rows = jnp.concatenate([tables(own), tables(other)], axis=0)
    mine = lax.dynamic_slice_in_dim(rows[:NEAR], lax.axis_index("z") * PX, PX, axis=0).astype(jnp.int32)
    slot = mine[:, 0:2].reshape(PX, ENTRIES)
    pattern = mine[:, 2:4].reshape(PX, ENTRIES)
    sent = lax.dynamic_slice_in_dim(rows[:, 4], core * 3 * PX, 3 * PX, axis=1).astype(jnp.int32)
    sender = lax.broadcasted_iota(jnp.int32, (PX, DEVICES), 1)
    counts = sent[:, 2 * PX : 3 * PX].T
    where = [
        jnp.where(k < counts, sender * OWNED + sent[:, k * PX : (k + 1) * PX].T, -1) for k in range(2)
    ]
    owner = slot // 2
    near = owner // (CORES * PX) * PX + owner % PX
    place = near + jnp.where(owner // PX % CORES == core, 0, NEAR)
    sender_at = lax.broadcasted_iota(jnp.int32, (PX, ENTRIES, DEVICES), 2)
    found = jnp.where(slot[:, :, None] % 2 == 0, where[0][:, None, :], where[1][:, None, :])
    block = jnp.sum(jnp.where(place[:, :, None] == sender_at, found, 0), axis=2)
    return jnp.where(block >= 0, pattern * TILES + block, ZERO_TILE).reshape(PX * ENTRIES)


def shifted(rows, left, right):
    wide = rows.astype(F32)
    column = lax.broadcasted_iota(jnp.int32, wide.shape, 0)
    last = wide.shape[0] - 1
    before = jnp.where(column == 0, jnp.broadcast_to(left, wide.shape), pltpu.roll(wide, 1, 0))
    after = jnp.where(column == last, jnp.broadcast_to(right, wide.shape), pltpu.roll(wide, last, 0))
    return before.astype(BF16), rows, after.astype(BF16)


def fill(taps_ref, row, cells, left_ref, right_ref):
    depth = cells.shape[-1]
    parts = shifted(cells, left_ref[row], right_ref[row])
    for k in range(3):
        taps_ref[row, :, k * depth : (k + 1) * depth] = parts[k]


def fill_all(taps_ref, cells_ref, top_ref, bottom_ref, left_ref, right_ref):
    count = cells_ref.shape[0]
    fill(taps_ref, 0, top_ref[0], left_ref, right_ref)

    def one(row, carry):
        fill(taps_ref, row + 1, cells_ref[row], left_ref, right_ref)
        return carry

    lax.fori_loop(0, count, one, 0)
    fill(taps_ref, count + 1, bottom_ref[0], left_ref, right_ref)


def taps_dot(taps_ref, weights_ref, first_row, count):
    columns, depth = taps_ref.shape[1], taps_ref.shape[2]
    total = None
    for row_off in range(3):
        rows = taps_ref[pl.ds(first_row + row_off, count)].reshape(count * columns, depth)
        product = dot(rows, weights_ref[row_off])
        total = product if total is None else total + product
    return total


STRIP = 8


def conv_kernel(cells_ref, top_ref, bottom_ref, left_ref, right_ref, weights_ref, out_ref, taps_ref):
    step = pl.program_id(0)

    @pl.when(step == 0)
    def _():
        fill_all(taps_ref, cells_ref, top_ref, bottom_ref, left_ref, right_ref)

    total = taps_dot(taps_ref, weights_ref, step * STRIP, STRIP)
    out_ref[...] = total.reshape(STRIP, COLUMNS, FINE).astype(BF16)


def in_hbm(array):
    return pltpu.with_memory_space_constraint(array, pltpu.HBM)


def whole(*shape):
    return pl.BlockSpec(shape, lambda i: (0,) * len(shape))


def conv_fine(cells, halo, weights):
    return pl.pallas_call(
        conv_kernel,
        grid=(ROWS // STRIP,),
        in_specs=[
            whole(ROWS, COLUMNS, FINE),
            whole(1, COLUMNS, FINE),
            whole(1, COLUMNS, FINE),
            whole(ROWS + 2, 1, FINE),
            whole(ROWS + 2, 1, FINE),
            whole(3, 3 * FINE, FINE),
        ],
        out_specs=pl.BlockSpec((STRIP, COLUMNS, FINE), lambda i: (i, 0, 0)),
        out_shape=pltpu.HBM((ROWS, COLUMNS, FINE), BF16),
        scratch_shapes=[pltpu.VMEM((ROWS + 2, COLUMNS, 3 * FINE), BF16)],
        compiler_params=pltpu.CompilerParams(vmem_limit_bytes=48 * MIB),
    )(in_hbm(cells), *halo, weights)


STRIPS = 2
ROW_TILES = COLUMNS // SUBTILE_COLUMNS


def first_kernel(blended_ref, lift_ref, conv_ref, cells_ref, first_ref, pooled_ref):
    cell = lax.broadcasted_iota(jnp.int32, (32, CELLS), 1)
    target = lax.broadcasted_iota(jnp.int32, (32, CELLS), 0)
    row = cell // SUBTILE_COLUMNS
    column = cell % SUBTILE_COLUMNS
    pool = jnp.where((row // 2) * 8 + column // 2 == target, 0.25, 0.0).astype(BF16)
    for strip in range(STRIPS):
        parts = []
        for pair in range(ROW_TILES // 2):
            start = (strip * ROW_TILES + 2 * pair) * SLOT
            both = blended_ref[:, start : start + 2 * SLOT, :].astype(F32)
            for half in range(2):
                part = both[:, half * SLOT : (half + 1) * SLOT, :]
                parts.append(part.reshape(PX * SLOT, CELLS).astype(BF16))
        lifted = lax.dot_general(
            jnp.concatenate(parts, axis=1), lift_ref[...], (((0,), (0,)), ((), ())), preferred_element_type=F32
        )
        rows = slice(strip * STRIP, (strip + 1) * STRIP)
        half_rows = slice(strip * STRIP // 2, (strip + 1) * STRIP // 2)
        for tile in range(ROW_TILES):
            columns = slice(tile * SUBTILE_COLUMNS, (tile + 1) * SUBTILE_COLUMNS)
            guidance = lifted[tile * CELLS : (tile + 1) * CELLS].astype(BF16).astype(F32)
            summed = conv_ref[rows, columns, :].astype(F32).reshape(CELLS, FINE) + guidance
            kept = cells_ref[rows, columns, :].reshape(CELLS, FINE).astype(F32)
            first = (kept + silu(summed)).astype(BF16)
            first_ref[rows, columns, :] = first.reshape(SUBTILE_ROWS, SUBTILE_COLUMNS, FINE)
            pooled = dot(pool, first).reshape(STRIP // 2, 8, FINE).astype(BF16)
            pooled_ref[half_rows, tile * 8 : (tile + 1) * 8, :] = pooled


def first_level(blended, lift, conv, cells):
    strip = pl.BlockSpec((STRIPS * STRIP, COLUMNS, FINE), lambda i: (i, 0, 0))
    return pl.pallas_call(
        first_kernel,
        grid=(ROWS // (STRIPS * STRIP),),
        in_specs=[
            pl.BlockSpec((PX, STRIPS * ROW_TILES * SLOT, CELLS), lambda i: (0, i, 0)),
            whole(PX * SLOT, FINE),
            strip,
            strip,
        ],
        out_specs=[strip, pl.BlockSpec((STRIPS * STRIP // 2, COLUMNS // 2, FINE), lambda i: (i, 0, 0))],
        out_shape=[
            pltpu.HBM((ROWS, COLUMNS, FINE), BF16),
            jax.ShapeDtypeStruct((ROWS // 2, COLUMNS // 2, FINE), BF16),
        ],
        compiler_params=pltpu.CompilerParams(vmem_limit_bytes=32 * MIB),
    )(blended, lift, in_hbm(conv), in_hbm(cells))


SECOND = 8


def second_kernel(
    pooled_ref, top_ref, bottom_ref, left_ref, right_ref, weights_ref, up_ref, first_ref, out_ref, taps_ref, spread_ref
):
    step = pl.program_id(0)

    @pl.when(step == 0)
    def _():
        fill_all(taps_ref, pooled_ref, top_ref, bottom_ref, left_ref, right_ref)

    second = silu(taps_dot(taps_ref, weights_ref, step * SECOND, SECOND)).astype(BF16)
    projected = dot(second, up_ref[...])
    half = COLUMNS // 2
    for lane in range(FINE // 128):
        part = projected[:, lane * 128 : (lane + 1) * 128]
        for side in range(2):
            spread_ref[lane, pl.ds(side, SECOND * half, stride=2), :] = part
    for lane in range(FINE // 128):
        lanes = slice(lane * 128, (lane + 1) * 128)
        for row in range(SECOND):
            added = spread_ref[lane, row * COLUMNS : (row + 1) * COLUMNS, :]
            for side in range(2):
                first = first_ref[2 * row + side, :, lanes].astype(F32)
                out_ref[2 * row + side, :, lanes] = (first + added).astype(BF16)


def second_level(pooled, halo, weights, up, first):
    strip = pl.BlockSpec((2 * SECOND, COLUMNS, FINE), lambda i: (i, 0, 0))
    return pl.pallas_call(
        second_kernel,
        grid=(ROWS // 2 // SECOND,),
        in_specs=[
            whole(ROWS // 2, COLUMNS // 2, FINE),
            whole(1, COLUMNS // 2, FINE),
            whole(1, COLUMNS // 2, FINE),
            whole(ROWS // 2 + 2, 1, FINE),
            whole(ROWS // 2 + 2, 1, FINE),
            whole(3, 3 * FINE, WIDE),
            whole(WIDE, FINE),
            strip,
        ],
        out_specs=strip,
        out_shape=jax.ShapeDtypeStruct((ROWS, COLUMNS, FINE), BF16),
        scratch_shapes=[
            pltpu.VMEM((ROWS // 2 + 2, COLUMNS // 2, 3 * FINE), BF16),
            pltpu.VMEM((FINE // 128, SECOND * COLUMNS, 128), F32),
        ],
        compiler_params=pltpu.CompilerParams(vmem_limit_bytes=48 * MIB),
    )(pooled, *halo, weights, up, in_hbm(first))


ROWS_AXES = ("z", "core")


def halo_rows(cells):
    down = [(i, i + 1) for i in range(PY - 1)]
    up = [(i + 1, i) for i in range(PY - 1)]
    return lax.ppermute(cells[-1:], ROWS_AXES, down), lax.ppermute(cells[:1], ROWS_AXES, up)


def halo_columns(cells, top, bottom):
    def column(at):
        return jnp.concatenate([top[:, at], cells[:, at], bottom[:, at]], axis=0)

    left = lax.ppermute(column(-1), "px", [(i, i + 1) for i in range(PX - 1)])
    right = lax.ppermute(column(0), "px", [(i + 1, i) for i in range(PX - 1)])
    return left[:, None].astype(F32), right[:, None].astype(F32)


def local(
    features,
    coarse,
    send_ids,
    send_counts,
    entry_slot,
    entry_weight_pattern,
    interpolation_weights,
    lift_weight,
    conv_a,
    conv_b,
    up_weight,
):
    above, below = halo_rows(features)
    ids = send_ids[0].reshape(Z, CORES, PX, 2).transpose(0, 1, 3, 2).reshape(Z, CORES, 2 * PX)
    sent = jnp.concatenate([ids, send_counts[0].reshape(Z, CORES, PX)], axis=2).reshape(Z, 1, CORES * 3 * PX)
    sent = jnp.pad(sent, ((0, 0), (0, 0), (0, CELLS - CORES * 3 * PX)))
    named = jnp.concatenate([entry_slot[0].reshape(2, CELLS), entry_weight_pattern[0].reshape(2, CELLS)], axis=0)
    named = jnp.broadcast_to(named[None], (Z, 4, CELLS))
    tables = jnp.concatenate([named, sent, jnp.zeros((Z, 3, CELLS), jnp.int32)], axis=1).astype(F32)
    outgoing = pack(coarse, tables).reshape(NEAR, OWNED * SLOT, CELLS)
    own = lax.all_to_all(outgoing, ("z", "px"), split_axis=0, concat_axis=0, tiled=True)
    other = lax.ppermute(own, "core", [(0, 1), (1, 0)])
    index = entry_index(own, other)
    index, above, below = lax.optimization_barrier((index, above, below))
    half = (NEAR * OWNED * SLOT, CELLS)
    parts = blend(index, own.reshape(half), other.reshape(half), interpolation_weights)
    blended = lax.all_to_all(
        parts.reshape(PX, SUBTILES * SLOT, CELLS), "px", split_axis=0, concat_axis=0, tiled=True
    )
    edges = (above, below, *halo_columns(features, above, below))
    conv = conv_fine(features, edges, conv_a.reshape(3, 3 * FINE, FINE))
    lift = jnp.pad(lift_weight, ((0, PX * PART - CHANNELS), (0, 0))).reshape(PX, PART, FINE)
    lift = jnp.pad(lift, ((0, 0), (0, SLOT - PART), (0, 0))).reshape(PX * SLOT, FINE)
    first, pooled = first_level(blended, lift, conv, features)
    above, below = halo_rows(pooled)
    edges = (above, below, *halo_columns(pooled, above, below))
    return second_level(pooled, edges, conv_b.reshape(3, 3 * FINE, WIDE), up_weight, first)


def solution(mesh):
    split = Mesh(mesh.devices.reshape(Z, CORES, PX), ("z", "core", "px"))
    every = ("z", "core", "px")
    placed = (
        P(ROWS_AXES, "px", None),
        P(every, None, None),
        P(every, None, None),
        P(every, None),
        P(every, None),
        P(every, None),
        P(),
        P(),
        P(),
        P(),
        P(),
    )
    return jax.shard_map(
        local, mesh=split, in_specs=placed, out_specs=P(ROWS_AXES, "px", None), check_vma=False
    )
```

```python
import functools

import jax
import jax.numpy as jnp
from jax import lax
from jax.experimental import pallas as pl
from jax.experimental.pallas import tpu as pltpu
from jax.sharding import Mesh
from jax.sharding import PartitionSpec as P

F32 = jnp.float32
BF16 = jnp.bfloat16
MIB = 1024 * 1024

SUBTILE_ENTRIES = 4
SUBTILE_ROWS = 8
SUBTILE_COLUMNS = 16
Z = 4
CORES = 2
PY = Z * CORES
PX = 16
NEAR = PY // CORES * PX
DEVICES = PY * PX
OWNED = 8
CELLS = 128
CHANNELS = 100
PART = 7
SLOT = 8
PATTERNS = 8
SUBTILES = 64
ENTRIES = SUBTILES * SUBTILE_ENTRIES
TILE_COLUMNS = 8
PART_ROWS = (SUBTILES + 2) * SLOT
ROWS = 64
COLUMNS = 128
FINE = 256
WIDE = 512
TILES = DEVICES * OWNED
ZERO_TILE = PATTERNS * TILES


def silu(v):
    return 0.5 * v * (1.0 + jnp.tanh(0.5 * v))


def in_hbm(array):
    return pltpu.with_memory_space_constraint(array, pltpu.HBM)


def in_vmem(array):
    return pltpu.with_memory_space_constraint(array, pltpu.VMEM)


def whole(*shape):
    return pl.BlockSpec(shape, lambda i: (0,) * len(shape))


def dot(a, b):
    return jnp.dot(a, b, preferred_element_type=F32)


def part_rows():
    row = lax.broadcasted_iota(jnp.int32, (PX * SLOT, CHANNELS), 0)
    channel = lax.broadcasted_iota(jnp.int32, (PX * SLOT, CHANNELS), 1)
    place = row % SLOT
    chosen = (channel == (row // SLOT) * PART + place) & (place < PART)
    return jnp.where(chosen, 1.0, 0.0).astype(BF16)


def pack_kernel(coarse_ref, ids_ref, counts_ref, slot_ref, pattern_ref, out_ref, wide_ref, parts_ref):
    @pl.when(pl.program_id(0) == 0)
    def _():
        wide_ref[...] = coarse_ref[...].astype(F32).reshape(CHANNELS * OWNED, CELLS)
        pick = part_rows()
        tables = [
            slot_ref[:, :CELLS],
            slot_ref[:, CELLS:],
            pattern_ref[:, :CELLS],
            pattern_ref[:, CELLS:],
            ids_ref[0:1],
            ids_ref[1:2],
            counts_ref[...],
            jnp.zeros((1, CELLS), jnp.int32),
        ]
        last = lax.broadcasted_iota(jnp.int32, (PX, SLOT, CELLS), 1) == PART
        for block in range(OWNED):
            cells = wide_ref[pl.ds(block, CHANNELS, stride=OWNED), :].astype(BF16)
            table = jnp.broadcast_to(tables[block].astype(F32)[None], (PX, SLOT, CELLS))
            part = dot(pick, cells).reshape(PX, SLOT, CELLS)
            parts_ref[:, block] = jnp.where(last, table, part)

    out_ref[0] = parts_ref[...].reshape(PX, OWNED * SLOT, CELLS).astype(BF16)


def pack(coarse, ids, counts, slot, pattern):
    return pl.pallas_call(
        pack_kernel,
        grid=(Z,),
        in_specs=[
            whole(CHANNELS, OWNED, CELLS),
            whole(2, DEVICES),
            whole(1, DEVICES),
            whole(1, ENTRIES),
            whole(1, ENTRIES),
        ],
        out_specs=pl.BlockSpec((1, PX, OWNED * SLOT, CELLS), lambda i: (i, 0, 0, 0)),
        out_shape=pltpu.HBM((Z, PX, OWNED * SLOT, CELLS), BF16),
        scratch_shapes=[pltpu.VMEM((CHANNELS * OWNED, CELLS), F32), pltpu.VMEM((PX, OWNED, SLOT, CELLS), F32)],
        compiler_params=pltpu.CompilerParams(vmem_limit_bytes=24 * MIB),
    )(*(in_hbm(array) for array in (coarse, ids, counts, slot, pattern)))


def find_entries(here_ref, own_ref, other_ref, rows_ref, table_ref):
    z, core = here_ref[0], here_ref[1]
    width = 2 * SLOT

    def table(ref, senders, block):
        count = NEAR if senders is None else PX
        where = slice(None) if senders is None else senders
        both = ref[where, block * SLOT : block * SLOT + width, :].astype(F32)
        rows_ref[: count * width] = both.reshape(count * width, CELLS)
        return [rows_ref[pl.ds(SLOT * k + PART, count, stride=width), :] for k in range(2)]

    def sent(block):
        pairs = zip(table(own_ref, None, block), table(other_ref, None, block))
        return [jnp.concatenate(pair, axis=0) for pair in pairs]

    def of_patches(values):
        table_ref[...] = values.T
        return table_ref[pl.ds(pl.multiple_of((CORES * z + core) * PX, PX), PX), :].astype(jnp.int32)

    ids = [of_patches(part) for part in sent(4)]
    counts = of_patches(sent(6)[0])
    sender = lax.broadcasted_iota(jnp.int32, (PX, DEVICES), 1)
    where = [jnp.where(k < counts, sender * OWNED + ids[k], -1) for k in range(2)]
    mine = pl.ds(pl.multiple_of(z * PX, PX), PX)
    slots = table(own_ref, mine, 0)
    patterns = table(own_ref, mine, 2)
    found = []
    for half in range(2):
        slot = slots[half].astype(jnp.int32)
        pattern = patterns[half].astype(jnp.int32)
        owner = slot // 2
        near = owner // (CORES * PX) * PX + owner % PX
        place = near + jnp.where(owner // PX % CORES == core, 0, NEAR)
        either = [jnp.take_along_axis(part, place, axis=1) for part in where]
        block = jnp.where(slot % 2 == 0, either[0], either[1])
        found.append(jnp.where(block >= 0, pattern * TILES + block, ZERO_TILE))
    return found


def blend_kernel(
    here_ref, own_ref, other_ref, weights_ref, out_ref, table_ref, rows_ref, sent_ref, beside_ref, found_ref, index_ref, sem
):
    chunk = 1024
    found = find_entries(here_ref, own_ref, other_ref, rows_ref, sent_ref)
    for half in range(2):
        found_ref[half] = found[half]
    copy = pltpu.make_async_copy(found_ref, index_ref, sem)
    copy.start()

    def multiply(blocks_ref, first, step):
        senders = pl.ds(step * (chunk // (OWNED * SLOT)), chunk // (OWNED * SLOT))
        part = blocks_ref[senders].reshape(chunk, CELLS)
        for pair in range(PATTERNS // 2):
            both = jnp.concatenate([weights_ref[2 * pair], weights_ref[2 * pair + 1]], axis=1)
            product = dot(part, both)
            for half in range(2):
                tiles = pl.ds((2 * pair + half) * TILES + first + step * (chunk // SLOT), chunk // SLOT)
                lanes = slice(half * CELLS, (half + 1) * CELLS)
                table_ref[tiles] = product[:, lanes].reshape(chunk // SLOT, SLOT, CELLS)

    for first, blocks_ref in ((0, own_ref), (TILES // 2, other_ref)):

        def one(step, carry):
            multiply(blocks_ref, first, step)
            return carry

        lax.fori_loop(0, TILES // 2 * SLOT // chunk, one, 0)
    table_ref[ZERO_TILE] = jnp.zeros((SLOT, CELLS), F32)

    copy.wait()

    def total(half, patch, entry):
        tile = [table_ref[index_ref[half, patch, entry + i]] for i in range(SUBTILE_ENTRIES)]
        return (tile[0] + tile[1]) + (tile[2] + tile[3])

    group = SUBTILES // 2

    def gather(patch, carry):
        for half in range(2):
            sums = [total(half, patch, k * SUBTILE_ENTRIES) for k in range(group)]
            for k in range(group):
                tile_row, tile_column = divmod(half * group + k, TILE_COLUMNS)
                if tile_column in (0, TILE_COLUMNS - 1):
                    side = 0 if tile_column else 1
                    at = pl.ds(pl.multiple_of(patch * SLOT, SLOT), SLOT)
                    beside_ref[side, at, tile_row * CELLS : (tile_row + 1) * CELLS] = sums[k]
            for k in range(0, group, 2):
                start = (half * group + k) * SLOT
                out_ref[patch, start : start + 2 * SLOT, :] = jnp.concatenate(sums[k : k + 2], axis=0).astype(BF16)
        return carry

    lax.fori_loop(0, PX, gather, 0)

    tall = TILE_COLUMNS * CELLS
    source = lax.broadcasted_iota(jnp.int32, (tall, CELLS), 0)
    lane = lax.broadcasted_iota(jnp.int32, (tall, CELLS), 1)
    row = lane % ROWS
    cell = (row // SUBTILE_ROWS) * CELLS + (row % SUBTILE_ROWS) * SUBTILE_COLUMNS + lane // ROWS
    moved = []
    for side, column in ((0, SUBTILE_COLUMNS - 2), (1, 0)):
        chosen = jnp.where(source == cell + column, 1.0, 0.0).astype(BF16)
        moved.append(dot(beside_ref[side].astype(BF16), chosen).reshape(PX, SLOT, CELLS))
    nothing = jnp.zeros((1, SLOT, CELLS), F32)
    left = jnp.concatenate([nothing, moved[0][: PX - 1]], axis=0)
    right = jnp.concatenate([moved[1][1:], nothing], axis=0)
    out_ref[:, SUBTILES * SLOT :, :] = jnp.concatenate([left, right], axis=1).astype(BF16)


def blend(here, own, other, weights):
    vmem = pl.BlockSpec(memory_space=pltpu.VMEM)
    return pl.pallas_call(
        blend_kernel,
        in_specs=[pl.BlockSpec(memory_space=pltpu.SMEM), vmem, vmem, vmem],
        out_specs=vmem,
        out_shape=pltpu.HBM((PX, PART_ROWS, CELLS), BF16),
        scratch_shapes=[
            pltpu.VMEM((ZERO_TILE + 1, SLOT, CELLS), F32),
            pltpu.VMEM((NEAR * 2 * SLOT, CELLS), F32),
            pltpu.VMEM((DEVICES, CELLS), F32),
            pltpu.VMEM((2, PX * SLOT, TILE_COLUMNS * CELLS), F32),
            pltpu.VMEM((2, PX, CELLS), jnp.int32),
            pltpu.SMEM((2, PX, CELLS), jnp.int32),
            pltpu.SemaphoreType.DMA,
        ],
        compiler_params=pltpu.CompilerParams(vmem_limit_bytes=44 * MIB),
    )(here, own, other, in_hbm(weights))


def shifted(rows, left, right):
    wide = rows.astype(F32)
    column = lax.broadcasted_iota(jnp.int32, wide.shape, 0)
    last = wide.shape[0] - 1
    before = jnp.where(column == 0, jnp.broadcast_to(left, wide.shape), pltpu.roll(wide, 1, 0))
    after = jnp.where(column == last, jnp.broadcast_to(right, wide.shape), pltpu.roll(wide, last, 0))
    return before.astype(BF16), rows, after.astype(BF16)


def put(taps_ref, row, parts):
    depth = parts[0].shape[-1]
    for k in range(3):
        taps_ref[row, :, k * depth : (k + 1) * depth] = parts[k]


def fill(taps_ref, row, cells, left_ref, right_ref):
    put(taps_ref, row, shifted(cells, left_ref[row], right_ref[row]))


def fill_all(taps_ref, cells_ref, top_ref, bottom_ref, left_ref, right_ref):
    count = cells_ref.shape[0]
    fill(taps_ref, 0, top_ref[0], left_ref, right_ref)

    def one(row, carry):
        fill(taps_ref, row + 1, cells_ref[row], left_ref, right_ref)
        return carry

    lax.fori_loop(0, count, one, 0)
    fill(taps_ref, count + 1, bottom_ref[0], left_ref, right_ref)


def taps_dot(taps_ref, weights_ref, first_row, count):
    columns, depth = taps_ref.shape[1], taps_ref.shape[2]
    total = None
    for row_off in range(3):
        rows = taps_ref[pl.ds(first_row + row_off, count)].reshape(count * columns, depth)
        product = dot(rows, weights_ref[row_off])
        total = product if total is None else total + product
    return total


STRIP = 8


EDGE = 16
REACH = 3


def edges_kernel(left_ref, right_ref, left_out, right_out, wide_ref):
    for cells_ref, out_ref, column in ((left_ref, left_out, 0), (right_ref, right_out, EDGE - REACH)):
        for lane in range(FINE // 128):
            lanes = slice(lane * 128, (lane + 1) * 128)
            wide_ref[...] = cells_ref[:, :, lanes].astype(F32).reshape(ROWS * EDGE, 128)
            for k in range(REACH):
                out_ref[k, :, lanes] = wide_ref[pl.ds(column + k, ROWS, stride=EDGE), :].astype(BF16)


def edge_columns(cells):
    cells = in_hbm(cells)
    columns = jax.ShapeDtypeStruct((REACH, ROWS, FINE), BF16)
    return pl.pallas_call(
        edges_kernel,
        grid=(1,),
        in_specs=[
            pl.BlockSpec((ROWS, EDGE, FINE), lambda i: (0, 0, 0)),
            pl.BlockSpec((ROWS, EDGE, FINE), lambda i: (0, COLUMNS // EDGE - 1, 0)),
        ],
        out_specs=[whole(REACH, ROWS, FINE)] * 2,
        out_shape=[columns, columns],
        scratch_shapes=[pltpu.VMEM((ROWS * EDGE, 128), F32)],
        compiler_params=pltpu.CompilerParams(vmem_limit_bytes=8 * MIB),
    )(cells, cells)


def strip_kernel(cells_ref, top_ref, weights_ref, out_ref, taps_ref):
    empty = jnp.zeros((1, FINE), F32)
    put(taps_ref, 0, shifted(top_ref[0], empty, empty))
    for row in range(STRIP + 1):
        put(taps_ref, row + 1, shifted(cells_ref[row], empty, empty))
    total = taps_dot(taps_ref, weights_ref, 0, STRIP)
    out_ref[...] = total.reshape(STRIP, COLUMNS, FINE).astype(BF16)


def conv_strip(cells, top, weights):
    return pl.pallas_call(
        strip_kernel,
        grid=(1,),
        in_specs=[whole(2 * STRIP, COLUMNS, FINE), whole(1, COLUMNS, FINE), whole(3, 3 * FINE, FINE)],
        out_specs=whole(STRIP, COLUMNS, FINE),
        out_shape=pltpu.HBM((STRIP, COLUMNS, FINE), BF16),
        scratch_shapes=[pltpu.VMEM((STRIP + 2, COLUMNS, 3 * FINE), BF16)],
        compiler_params=pltpu.CompilerParams(vmem_limit_bytes=16 * MIB),
    )(in_hbm(cells), top, in_hbm(weights))


def conv_kernel(cells_ref, bottom_ref, weights_ref, strip_ref, out_ref, taps_ref):
    step = pl.program_id(0)

    @pl.when(step == 0)
    def _():
        empty = jnp.zeros((1, FINE), F32)

        def one(row, carry):
            put(taps_ref, row + 1, shifted(cells_ref[row], empty, empty))
            return carry

        lax.fori_loop(STRIP - 1, ROWS, one, 0)
        put(taps_ref, ROWS + 1, shifted(bottom_ref[0], empty, empty))
        out_ref[...] = strip_ref[...]

    @pl.when(step > 0)
    def _():
        total = taps_dot(taps_ref, weights_ref, step * STRIP, STRIP)
        out_ref[...] = total.reshape(STRIP, COLUMNS, FINE).astype(BF16)


def conv_inside(cells, bottom, weights, strip):
    return pl.pallas_call(
        conv_kernel,
        grid=(ROWS // STRIP,),
        in_specs=[
            whole(ROWS, COLUMNS, FINE),
            whole(1, COLUMNS, FINE),
            whole(3, 3 * FINE, FINE),
            whole(STRIP, COLUMNS, FINE),
        ],
        out_specs=pl.BlockSpec((STRIP, COLUMNS, FINE), lambda i: (i, 0, 0)),
        out_shape=pltpu.HBM((ROWS, COLUMNS, FINE), BF16),
        scratch_shapes=[pltpu.VMEM((ROWS + 2, COLUMNS, 3 * FINE), BF16)],
        compiler_params=pltpu.CompilerParams(vmem_limit_bytes=40 * MIB),
    )(in_hbm(cells), bottom, in_hbm(weights), strip)


def sides_kernel(before_ref, after_ref, first_ref, last_ref, weights_ref, sides_ref, beside_ref):
    def taps(ref, k):
        ends = [ref[k, ROWS + end : ROWS + end + 1, :].astype(F32) for end in range(2)]
        return jnp.concatenate(shifted(ref[k, :ROWS, :], *ends), axis=1)

    left = [taps(before_ref, k) for k in range(REACH)] + [taps(first_ref, 0)]
    right = [taps(last_ref, REACH - 1)] + [taps(after_ref, k) for k in range(REACH)]
    total = jnp.zeros((4 * ROWS, FINE), F32)
    for col_off in range(3):
        start = col_off * FINE
        part = jnp.concatenate([weights_ref[row_off, start : start + FINE, :] for row_off in range(3)], axis=0)
        if col_off == 0:
            sides_ref[0] = dot(left[2], part).reshape(ROWS, 1, FINE)
        if col_off == 2:
            sides_ref[1] = dot(right[1], part).reshape(ROWS, 1, FINE)
        rows = [left[col_off], left[col_off + 1], right[col_off], right[col_off + 1]]
        total = total + dot(jnp.concatenate(rows, axis=0), part)
    beside_ref[...] = total.reshape(2, 2 * ROWS, FINE)


def conv_sides(before, after, first, last, weights):
    column = whole(REACH, ROWS + 2, FINE)
    return pl.pallas_call(
        sides_kernel,
        grid=(1,),
        in_specs=[column] * 4 + [whole(3, 3 * FINE, FINE)],
        out_specs=[whole(2, ROWS, 1, FINE), whole(2, 2 * ROWS, FINE)],
        out_shape=[
            jax.ShapeDtypeStruct((2, ROWS, 1, FINE), F32),
            jax.ShapeDtypeStruct((2, 2 * ROWS, FINE), F32),
        ],
        compiler_params=pltpu.CompilerParams(vmem_limit_bytes=16 * MIB),
    )(before, after, first, last, in_hbm(weights))


STRIPS = 2
ROW_TILES = COLUMNS // SUBTILE_COLUMNS


def pool_of(group):
    return jnp.where(group == lax.broadcasted_iota(jnp.int32, group.shape, 0), 0.25, 0.0).astype(BF16)


def lifted_of(parts, lift):
    rows = [part.reshape(PX * SLOT, CELLS).astype(BF16) for part in parts]
    return lax.dot_general(
        jnp.concatenate(rows, axis=1), lift, (((0,), (0,)), ((), ())), preferred_element_type=F32
    ).astype(BF16)


def first_of(kept, conv, guidance):
    return (kept.astype(F32) + silu(conv + guidance.astype(F32))).astype(BF16)


def first_kernel(
    here_ref,
    blended_ref,
    blended_beside_ref,
    lift_ref,
    conv_ref,
    cells_ref,
    sides_ref,
    conv_beside_ref,
    before_ref,
    after_ref,
    first_ref,
    pooled_ref,
    pooled_beside_ref,
):
    lift = dot(part_rows(), lift_ref[...]).astype(BF16)
    cell = lax.broadcasted_iota(jnp.int32, (32, CELLS), 1)

    @pl.when(pl.program_id(0) == 0)
    def _():
        pool = pool_of(cell % ROWS // 2)
        both = blended_beside_ref[...].astype(F32)
        lifted = lifted_of([both[:, side * SLOT : (side + 1) * SLOT, :] for side in range(2)], lift)
        kept = [
            jnp.concatenate([before_ref[k, :ROWS, :] for k in (1, 2)], axis=0),
            jnp.concatenate([after_ref[k, :ROWS, :] for k in (0, 1)], axis=0),
        ]
        inside = [here_ref[2] > 0, here_ref[2] < PX - 1]
        for side in range(2):
            guidance = lifted[side * CELLS : (side + 1) * CELLS]
            first = first_of(kept[side], conv_beside_ref[side], guidance)
            pooled_beside_ref[side] = jnp.where(inside[side], dot(pool, first), 0.0).astype(BF16)

    row = cell // SUBTILE_COLUMNS
    column = cell % SUBTILE_COLUMNS
    pool = pool_of((row // 2) * 8 + column // 2)
    at = lax.broadcasted_iota(jnp.int32, (STRIP, SUBTILE_COLUMNS, FINE), 1)
    for strip in range(STRIPS):
        parts = []
        for pair in range(ROW_TILES // 2):
            start = (strip * ROW_TILES + 2 * pair) * SLOT
            both = blended_ref[:, start : start + 2 * SLOT, :].astype(F32)
            parts += [both[:, half * SLOT : (half + 1) * SLOT, :] for half in range(2)]
        lifted = lifted_of(parts, lift)
        rows = slice(strip * STRIP, (strip + 1) * STRIP)
        half_rows = slice(strip * STRIP // 2, (strip + 1) * STRIP // 2)
        for tile in range(ROW_TILES):
            columns = slice(tile * SUBTILE_COLUMNS, (tile + 1) * SUBTILE_COLUMNS)
            conv = conv_ref[rows, columns, :].astype(F32)
            if tile == 0:
                conv = conv + jnp.where(at == 0, sides_ref[0, rows], 0.0)
            if tile == ROW_TILES - 1:
                conv = conv + jnp.where(at == SUBTILE_COLUMNS - 1, sides_ref[1, rows], 0.0)
            kept = cells_ref[rows, columns, :].reshape(CELLS, FINE)
            first = first_of(kept, conv.reshape(CELLS, FINE), lifted[tile * CELLS : (tile + 1) * CELLS])
            first_ref[rows, columns, :] = first.reshape(SUBTILE_ROWS, SUBTILE_COLUMNS, FINE)
            pooled = dot(pool, first).reshape(STRIP // 2, 8, FINE).astype(BF16)
            pooled_ref[half_rows, tile * 8 : (tile + 1) * 8, :] = pooled


def first_level(here, blended, lift, conv, cells, sides, conv_beside, before, after):
    count = STRIPS * STRIP
    strip = pl.BlockSpec((count, COLUMNS, FINE), lambda i: (i, 0, 0))
    beside = pl.BlockSpec((PX, 2 * SLOT, CELLS), lambda i: (0, SUBTILES // 2, 0))
    return pl.pallas_call(
        first_kernel,
        grid=(ROWS // count,),
        in_specs=[
            pl.BlockSpec(memory_space=pltpu.SMEM),
            pl.BlockSpec((PX, STRIPS * ROW_TILES * SLOT, CELLS), lambda i: (0, i, 0)),
            beside,
            whole(CHANNELS, FINE),
            strip,
            strip,
            pl.BlockSpec((2, count, 1, FINE), lambda i: (0, i, 0, 0)),
            whole(2, 2 * ROWS, FINE),
            whole(REACH, ROWS + 2, FINE),
            whole(REACH, ROWS + 2, FINE),
        ],
        out_specs=[
            strip,
            pl.BlockSpec((count // 2, COLUMNS // 2, FINE), lambda i: (i, 0, 0)),
            whole(2, ROWS // 2, FINE),
        ],
        out_shape=[
            pltpu.VMEM((ROWS, COLUMNS, FINE), BF16),
            jax.ShapeDtypeStruct((ROWS // 2, COLUMNS // 2, FINE), BF16),
            jax.ShapeDtypeStruct((2, ROWS // 2, FINE), BF16),
        ],
        compiler_params=pltpu.CompilerParams(vmem_limit_bytes=32 * MIB),
    )(here, blended, blended, in_hbm(lift), in_hbm(conv), in_hbm(cells), sides, conv_beside, before, after)


SECOND = 8


def second_kernel(
    pooled_ref, top_ref, bottom_ref, left_ref, right_ref, weights_ref, up_ref, first_ref, out_ref, taps_ref, spread_ref
):
    step = pl.program_id(0)

    @pl.when(step == 0)
    def _():
        fill_all(taps_ref, pooled_ref, top_ref, bottom_ref, left_ref, right_ref)

    second = silu(taps_dot(taps_ref, weights_ref, step * SECOND, SECOND)).astype(BF16)
    projected = dot(second, up_ref[...])
    half = COLUMNS // 2
    for lane in range(FINE // 128):
        part = projected[:, lane * 128 : (lane + 1) * 128]
        for side in range(2):
            spread_ref[lane, pl.ds(side, SECOND * half, stride=2), :] = part
    for lane in range(FINE // 128):
        lanes = slice(lane * 128, (lane + 1) * 128)
        for row in range(SECOND):
            added = spread_ref[lane, row * COLUMNS : (row + 1) * COLUMNS, :]
            for side in range(2):
                first = first_ref[2 * row + side, :, lanes].astype(F32)
                out_ref[2 * row + side, :, lanes] = (first + added).astype(BF16)


def second_level(pooled, halo, weights, up, first):
    strip = pl.BlockSpec((2 * SECOND, COLUMNS, FINE), lambda i: (i, 0, 0))
    return pl.pallas_call(
        second_kernel,
        grid=(ROWS // 2 // SECOND,),
        in_specs=[
            whole(ROWS // 2, COLUMNS // 2, FINE),
            whole(1, COLUMNS // 2, FINE),
            whole(1, COLUMNS // 2, FINE),
            whole(ROWS // 2 + 2, 1, FINE),
            whole(ROWS // 2 + 2, 1, FINE),
            whole(3, 3 * FINE, WIDE),
            whole(WIDE, FINE),
            strip,
        ],
        out_specs=strip,
        out_shape=jax.ShapeDtypeStruct((ROWS, COLUMNS, FINE), BF16),
        scratch_shapes=[
            pltpu.VMEM((ROWS // 2 + 2, COLUMNS // 2, 3 * FINE), BF16),
            pltpu.VMEM((FINE // 128, SECOND * COLUMNS, 128), F32),
        ],
        compiler_params=pltpu.CompilerParams(vmem_limit_bytes=48 * MIB),
    )(pooled, *halo, weights, up, in_vmem(first))


ROWS_AXES = ("z", "core")


def from_rows(last, first):
    down = [(i, i + 1) for i in range(PY - 1)]
    up = [(i + 1, i) for i in range(PY - 1)]
    return lax.ppermute(last, ROWS_AXES, down), lax.ppermute(first, ROWS_AXES, up)


def from_columns(last, first):
    return (
        lax.ppermute(last, "px", [(i, i + 1) for i in range(PX - 1)]),
        lax.ppermute(first, "px", [(i + 1, i) for i in range(PX - 1)]),
    )


def local(
    features,
    coarse,
    send_ids,
    send_counts,
    entry_slot,
    entry_weight_pattern,
    interpolation_weights,
    lift_weight,
    conv_a,
    conv_b,
    up_weight,
):
    here = jnp.stack([lax.axis_index(axis) for axis in ("z", "core", "px")]).astype(jnp.int32)
    outgoing = pack(coarse.transpose(1, 0, 2), send_ids[0].T, send_counts, entry_slot, entry_weight_pattern)
    outgoing, cells = lax.optimization_barrier((outgoing, features))
    own = lax.all_to_all(
        outgoing.reshape(NEAR, OWNED * SLOT, CELLS), ("z", "px"), split_axis=0, concat_axis=0, tiled=True
    )
    above, below = from_rows(cells[-1:], cells[:1])
    weights = conv_a.reshape(3, 3 * FINE, FINE)
    strip = conv_strip(cells, above, weights)
    first_columns, last_columns = edge_columns(cells)
    own, strip, above, below = lax.optimization_barrier((own, strip, above, below))
    other = lax.ppermute(own, "core", [(0, 1), (1, 0)])
    parts = blend(here, own, other, interpolation_weights)
    parts, strip, above, below = lax.optimization_barrier((parts, strip, above, below))
    blended = lax.all_to_all(parts, "px", split_axis=0, concat_axis=0, tiled=True)

    def with_ends(columns, start):
        ends = [row[:, start : start + REACH].transpose(1, 0, 2) for row in (above, below)]
        return jnp.concatenate([columns, *ends], axis=1)

    first_columns = with_ends(first_columns, 0)
    last_columns = with_ends(last_columns, COLUMNS - REACH)
    before, after = from_columns(last_columns, first_columns)
    conv = conv_inside(cells, below, weights, strip)
    sides, conv_beside = conv_sides(before, after, first_columns, last_columns, weights)
    first, pooled, pooled_beside = first_level(
        here, blended, lift_weight, conv, features, sides, conv_beside, before, after
    )

    def wide(row):
        return jnp.concatenate([pooled[row], pooled_beside[:, row]], axis=0)

    half = COLUMNS // 2
    above, below = from_rows(wide(ROWS // 2 - 1), wide(0))
    columns = [
        jnp.concatenate([above[half + side][None], pooled_beside[side], below[half + side][None]], axis=0)
        for side in range(2)
    ]
    edges = (above[None, :half], below[None, :half], *(column[:, None].astype(F32) for column in columns))
    return second_level(pooled, edges, conv_b.reshape(3, 3 * FINE, WIDE), up_weight, first)


def solution(mesh):
    split = Mesh(mesh.devices.reshape(Z, CORES, PX), ("z", "core", "px"))
    every = ("z", "core", "px")
    placed = (
        P(ROWS_AXES, "px", None),
        P(every, None, None),
        P(every, None, None),
        P(every, None),
        P(every, None),
        P(every, None),
        P(),
        P(),
        P(),
        P(),
        P(),
    )
    return jax.shard_map(
        local, mesh=split, in_specs=placed, out_specs=P(ROWS_AXES, "px", None), check_vma=False
    )
```

```python
import functools

import jax
import jax.numpy as jnp
from jax import lax
from jax.experimental import pallas as pl
from jax.experimental.pallas import tpu as pltpu
from jax.sharding import Mesh
from jax.sharding import PartitionSpec as P

F32 = jnp.float32
BF16 = jnp.bfloat16
MIB = 1024 * 1024

SUBTILE_ENTRIES = 4
SUBTILE_ROWS = 8
SUBTILE_COLUMNS = 16
Z = 4
CORES = 2
PY = Z * CORES
PX = 16
NEAR = PY // CORES * PX
DEVICES = PY * PX
OWNED = 8
CELLS = 128
CHANNELS = 100
PART = 7
SLOT = 8
PATTERNS = 8
SUBTILES = 64
ENTRIES = SUBTILES * SUBTILE_ENTRIES
TILE_COLUMNS = 8
PART_ROWS = (SUBTILES + 2) * SLOT
ROWS = 64
COLUMNS = 128
FINE = 256
WIDE = 512
TILES = DEVICES * OWNED
ZERO_TILE = PATTERNS * TILES


def silu(v):
    return 0.5 * v * (1.0 + jnp.tanh(0.5 * v))


def in_hbm(array):
    return pltpu.with_memory_space_constraint(array, pltpu.HBM)


def in_vmem(array):
    return pltpu.with_memory_space_constraint(array, pltpu.VMEM)


def whole(*shape):
    return pl.BlockSpec(shape, lambda i: (0,) * len(shape))


def dot(a, b):
    return jnp.dot(a, b, preferred_element_type=F32)


def part_rows():
    row = lax.broadcasted_iota(jnp.int32, (PX * SLOT, CHANNELS), 0)
    channel = lax.broadcasted_iota(jnp.int32, (PX * SLOT, CHANNELS), 1)
    place = row % SLOT
    chosen = (channel == (row // SLOT) * PART + place) & (place < PART)
    return jnp.where(chosen, 1.0, 0.0).astype(BF16)


def pack_kernel(coarse_ref, ids_ref, counts_ref, slot_ref, pattern_ref, out_ref, wide_ref, parts_ref):
    @pl.when(pl.program_id(0) == 0)
    def _():
        wide_ref[...] = coarse_ref[...].astype(F32).reshape(CHANNELS * OWNED, CELLS)
        pick = part_rows()
        tables = [
            slot_ref[:, :CELLS],
            slot_ref[:, CELLS:],
            pattern_ref[:, :CELLS],
            pattern_ref[:, CELLS:],
            ids_ref[0:1],
            ids_ref[1:2],
            counts_ref[...],
            jnp.zeros((1, CELLS), jnp.int32),
        ]
        last = lax.broadcasted_iota(jnp.int32, (PX, SLOT, CELLS), 1) == PART
        for block in range(OWNED):
            cells = wide_ref[pl.ds(block, CHANNELS, stride=OWNED), :].astype(BF16)
            table = jnp.broadcast_to(tables[block].astype(F32)[None], (PX, SLOT, CELLS))
            part = dot(pick, cells).reshape(PX, SLOT, CELLS)
            parts_ref[:, block] = jnp.where(last, table, part)

    out_ref[0] = parts_ref[...].reshape(PX, OWNED * SLOT, CELLS).astype(BF16)


def pack(coarse, ids, counts, slot, pattern):
    return pl.pallas_call(
        pack_kernel,
        grid=(Z,),
        in_specs=[
            whole(CHANNELS, OWNED, CELLS),
            whole(2, DEVICES),
            whole(1, DEVICES),
            whole(1, ENTRIES),
            whole(1, ENTRIES),
        ],
        out_specs=pl.BlockSpec((1, PX, OWNED * SLOT, CELLS), lambda i: (i, 0, 0, 0)),
        out_shape=pltpu.HBM((Z, PX, OWNED * SLOT, CELLS), BF16),
        scratch_shapes=[pltpu.VMEM((CHANNELS * OWNED, CELLS), F32), pltpu.VMEM((PX, OWNED, SLOT, CELLS), F32)],
        compiler_params=pltpu.CompilerParams(vmem_limit_bytes=24 * MIB),
    )(*(in_hbm(array) for array in (coarse, ids, counts, slot, pattern)))


def find_entries(here_ref, own_ref, other_ref, rows_ref, table_ref):
    z, core = here_ref[0], here_ref[1]
    width = 2 * SLOT

    def table(ref, senders, block):
        count = NEAR if senders is None else PX
        where = slice(None) if senders is None else senders
        both = ref[where, block * SLOT : block * SLOT + width, :].astype(F32)
        rows_ref[: count * width] = both.reshape(count * width, CELLS)
        return [rows_ref[pl.ds(SLOT * k + PART, count, stride=width), :] for k in range(2)]

    def sent(block):
        pairs = zip(table(own_ref, None, block), table(other_ref, None, block))
        return [jnp.concatenate(pair, axis=0) for pair in pairs]

    def of_patches(values):
        table_ref[...] = values.T
        return table_ref[pl.ds(pl.multiple_of((CORES * z + core) * PX, PX), PX), :].astype(jnp.int32)

    ids = [of_patches(part) for part in sent(4)]
    counts = of_patches(sent(6)[0])
    sender = lax.broadcasted_iota(jnp.int32, (PX, DEVICES), 1)
    where = [jnp.where(k < counts, sender * OWNED + ids[k], -1) for k in range(2)]
    mine = pl.ds(pl.multiple_of(z * PX, PX), PX)
    slots = table(own_ref, mine, 0)
    patterns = table(own_ref, mine, 2)
    found = []
    for half in range(2):
        slot = slots[half].astype(jnp.int32)
        pattern = patterns[half].astype(jnp.int32)
        owner = slot // 2
        near = owner // (CORES * PX) * PX + owner % PX
        place = near + jnp.where(owner // PX % CORES == core, 0, NEAR)
        either = [jnp.take_along_axis(part, place, axis=1) for part in where]
        block = jnp.where(slot % 2 == 0, either[0], either[1])
        found.append(jnp.where(block >= 0, pattern * TILES + block, ZERO_TILE))
    return found


def blend_kernel(
    here_ref, own_ref, other_ref, weights_ref, out_ref, table_ref, rows_ref, sent_ref, beside_ref, found_ref, index_ref, sem
):
    chunk = 1024
    found = find_entries(here_ref, own_ref, other_ref, rows_ref, sent_ref)
    for half in range(2):
        found_ref[half] = found[half]
    copy = pltpu.make_async_copy(found_ref, index_ref, sem)
    copy.start()

    def multiply(blocks_ref, first, step):
        senders = pl.ds(step * (chunk // (OWNED * SLOT)), chunk // (OWNED * SLOT))
        part = blocks_ref[senders].reshape(chunk, CELLS)
        for pair in range(PATTERNS // 2):
            both = jnp.concatenate([weights_ref[2 * pair], weights_ref[2 * pair + 1]], axis=1)
            product = dot(part, both)
            for half in range(2):
                tiles = pl.ds((2 * pair + half) * TILES + first + step * (chunk // SLOT), chunk // SLOT)
                lanes = slice(half * CELLS, (half + 1) * CELLS)
                table_ref[tiles] = product[:, lanes].reshape(chunk // SLOT, SLOT, CELLS)

    for first, blocks_ref in ((0, own_ref), (TILES // 2, other_ref)):

        def one(step, carry):
            multiply(blocks_ref, first, step)
            return carry

        lax.fori_loop(0, TILES // 2 * SLOT // chunk, one, 0)
    table_ref[ZERO_TILE] = jnp.zeros((SLOT, CELLS), F32)

    copy.wait()

    def total(half, patch, entry):
        tile = [table_ref[index_ref[half, patch, entry + i]] for i in range(SUBTILE_ENTRIES)]
        return (tile[0] + tile[1]) + (tile[2] + tile[3])

    group = SUBTILES // 2

    def gather(patch, carry):
        for half in range(2):
            sums = [total(half, patch, k * SUBTILE_ENTRIES) for k in range(group)]
            for k in range(group):
                tile_row, tile_column = divmod(half * group + k, TILE_COLUMNS)
                if tile_column in (0, TILE_COLUMNS - 1):
                    side = 0 if tile_column else 1
                    at = pl.ds(pl.multiple_of(patch * SLOT, SLOT), SLOT)
                    beside_ref[side, at, tile_row * CELLS : (tile_row + 1) * CELLS] = sums[k]
            for k in range(0, group, 2):
                start = (half * group + k) * SLOT
                out_ref[patch, start : start + 2 * SLOT, :] = jnp.concatenate(sums[k : k + 2], axis=0).astype(BF16)
        return carry

    lax.fori_loop(0, PX, gather, 0)

    tall = TILE_COLUMNS * CELLS
    source = lax.broadcasted_iota(jnp.int32, (tall, CELLS), 0)
    lane = lax.broadcasted_iota(jnp.int32, (tall, CELLS), 1)
    row = lane % ROWS
    cell = (row // SUBTILE_ROWS) * CELLS + (row % SUBTILE_ROWS) * SUBTILE_COLUMNS + lane // ROWS
    moved = []
    for side, column in ((0, SUBTILE_COLUMNS - 2), (1, 0)):
        chosen = jnp.where(source == cell + column, 1.0, 0.0).astype(BF16)
        moved.append(dot(beside_ref[side].astype(BF16), chosen).reshape(PX, SLOT, CELLS))
    nothing = jnp.zeros((1, SLOT, CELLS), F32)
    left = jnp.concatenate([nothing, moved[0][: PX - 1]], axis=0)
    right = jnp.concatenate([moved[1][1:], nothing], axis=0)
    out_ref[:, SUBTILES * SLOT :, :] = jnp.concatenate([left, right], axis=1).astype(BF16)


def blend(here, own, other, weights):
    vmem = pl.BlockSpec(memory_space=pltpu.VMEM)
    return pl.pallas_call(
        blend_kernel,
        in_specs=[pl.BlockSpec(memory_space=pltpu.SMEM), vmem, vmem, vmem],
        out_specs=vmem,
        out_shape=pltpu.HBM((PX, PART_ROWS, CELLS), BF16),
        scratch_shapes=[
            pltpu.VMEM((ZERO_TILE + 1, SLOT, CELLS), F32),
            pltpu.VMEM((NEAR * 2 * SLOT, CELLS), F32),
            pltpu.VMEM((DEVICES, CELLS), F32),
            pltpu.VMEM((2, PX * SLOT, TILE_COLUMNS * CELLS), F32),
            pltpu.VMEM((2, PX, CELLS), jnp.int32),
            pltpu.SMEM((2, PX, CELLS), jnp.int32),
            pltpu.SemaphoreType.DMA,
        ],
        compiler_params=pltpu.CompilerParams(vmem_limit_bytes=44 * MIB),
    )(here, own, other, in_hbm(weights))


def shifted(rows, left, right):
    wide = rows.astype(F32)
    column = lax.broadcasted_iota(jnp.int32, wide.shape, 0)
    last = wide.shape[0] - 1
    before = jnp.where(column == 0, jnp.broadcast_to(left, wide.shape), pltpu.roll(wide, 1, 0))
    after = jnp.where(column == last, jnp.broadcast_to(right, wide.shape), pltpu.roll(wide, last, 0))
    return before.astype(BF16), rows, after.astype(BF16)


def put(taps_ref, row, parts):
    depth = parts[0].shape[-1]
    for k in range(3):
        taps_ref[row, :, k * depth : (k + 1) * depth] = parts[k]


def fill(taps_ref, row, cells, left_ref, right_ref):
    put(taps_ref, row, shifted(cells, left_ref[row], right_ref[row]))


def fill_all(taps_ref, cells_ref, top_ref, bottom_ref, left_ref, right_ref):
    count = cells_ref.shape[0]
    fill(taps_ref, 0, top_ref[0], left_ref, right_ref)

    def one(row, carry):
        fill(taps_ref, row + 1, cells_ref[row], left_ref, right_ref)
        return carry

    lax.fori_loop(0, count, one, 0)
    fill(taps_ref, count + 1, bottom_ref[0], left_ref, right_ref)


def taps_dot(taps_ref, weights_ref, first_row, count):
    columns, depth = taps_ref.shape[1], taps_ref.shape[2]
    total = None
    for row_off in range(3):
        rows = taps_ref[pl.ds(first_row + row_off, count)].reshape(count * columns, depth)
        product = dot(rows, weights_ref[row_off])
        total = product if total is None else total + product
    return total


STRIP = 8


EDGE = 16
REACH = 3
LONG = COLUMNS + 16


def edges_kernel(left_ref, right_ref, left_out, right_out, wide_ref):
    for cells_ref, out_ref, column in ((left_ref, left_out, 0), (right_ref, right_out, EDGE - REACH)):
        for lane in range(FINE // 128):
            lanes = slice(lane * 128, (lane + 1) * 128)
            wide_ref[...] = cells_ref[:, :, lanes].astype(F32).reshape(ROWS * EDGE, 128)
            for k in range(REACH):
                out_ref[k, :, lanes] = wide_ref[pl.ds(column + k, ROWS, stride=EDGE), :].astype(BF16)


def edge_columns(cells):
    cells = in_hbm(cells)
    columns = jax.ShapeDtypeStruct((REACH, ROWS, FINE), BF16)
    return pl.pallas_call(
        edges_kernel,
        grid=(1,),
        in_specs=[
            pl.BlockSpec((ROWS, EDGE, FINE), lambda i: (0, 0, 0)),
            pl.BlockSpec((ROWS, EDGE, FINE), lambda i: (0, COLUMNS // EDGE - 1, 0)),
        ],
        out_specs=[whole(REACH, ROWS, FINE)] * 2,
        out_shape=[columns, columns],
        scratch_shapes=[pltpu.VMEM((ROWS * EDGE, 128), F32)],
        compiler_params=pltpu.CompilerParams(vmem_limit_bytes=8 * MIB),
    )(cells, cells)


INNER = 1


def strip_kernel(cells_ref, weights_ref, out_ref, taps_ref):
    empty = jnp.zeros((1, FINE), F32)
    for row in range(STRIP + 2):
        put(taps_ref, row, shifted(cells_ref[INNER * STRIP - 1 + row], empty, empty))
    total = taps_dot(taps_ref, weights_ref, 0, STRIP)
    out_ref[...] = total.reshape(STRIP, COLUMNS, FINE).astype(BF16)


def conv_strip(cells, weights):
    return pl.pallas_call(
        strip_kernel,
        grid=(1,),
        in_specs=[whole((INNER + 2) * STRIP, COLUMNS, FINE), whole(3, 3 * FINE, FINE)],
        out_specs=whole(STRIP, COLUMNS, FINE),
        out_shape=pltpu.HBM((STRIP, COLUMNS, FINE), BF16),
        scratch_shapes=[pltpu.VMEM((STRIP + 2, COLUMNS, 3 * FINE), BF16)],
        compiler_params=pltpu.CompilerParams(vmem_limit_bytes=16 * MIB),
    )(in_hbm(cells), in_hbm(weights))


def conv_kernel(cells_ref, above_ref, below_ref, weights_ref, strip_ref, out_ref, taps_ref):
    step = pl.program_id(0)

    @pl.when(step == 0)
    def _():
        empty = jnp.zeros((1, FINE), F32)

        def one(row, carry):
            put(taps_ref, row + 1, shifted(cells_ref[row], empty, empty))
            return carry

        lax.fori_loop(0, ROWS, one, 0)
        put(taps_ref, 0, shifted(above_ref[:COLUMNS], empty, empty))
        put(taps_ref, ROWS + 1, shifted(below_ref[:COLUMNS], empty, empty))

    @pl.when(step == INNER)
    def _():
        out_ref[...] = strip_ref[...]

    @pl.when(step != INNER)
    def _():
        total = taps_dot(taps_ref, weights_ref, step * STRIP, STRIP)
        out_ref[...] = total.reshape(STRIP, COLUMNS, FINE).astype(BF16)


def conv_inside(cells, above, below, weights, strip):
    return pl.pallas_call(
        conv_kernel,
        grid=(ROWS // STRIP,),
        in_specs=[
            whole(ROWS, COLUMNS, FINE),
            whole(LONG, FINE),
            whole(LONG, FINE),
            whole(3, 3 * FINE, FINE),
            whole(STRIP, COLUMNS, FINE),
        ],
        out_specs=pl.BlockSpec((STRIP, COLUMNS, FINE), lambda i: (i, 0, 0)),
        out_shape=pltpu.HBM((ROWS, COLUMNS, FINE), BF16),
        scratch_shapes=[pltpu.VMEM((ROWS + 2, COLUMNS, 3 * FINE), BF16)],
        compiler_params=pltpu.CompilerParams(vmem_limit_bytes=40 * MIB),
    )(in_hbm(cells), above, below, in_hbm(weights), strip)


def sides_kernel(
    before_ref, after_ref, first_ref, last_ref, above_ref, below_ref, weights_ref, sides_ref, beside_ref
):
    def taps(ref, k, at):
        ends = [row_ref[at : at + 1, :].astype(F32) for row_ref in (above_ref, below_ref)]
        return jnp.concatenate(shifted(ref[k], *ends), axis=1)

    left = [taps(before_ref, k, COLUMNS + k) for k in range(REACH)] + [taps(first_ref, 0, 0)]
    right = [taps(last_ref, REACH - 1, COLUMNS - 1)]
    right += [taps(after_ref, k, COLUMNS + REACH + k) for k in range(REACH)]
    total = jnp.zeros((4 * ROWS, FINE), F32)
    for col_off in range(3):
        start = col_off * FINE
        part = jnp.concatenate([weights_ref[row_off, start : start + FINE, :] for row_off in range(3)], axis=0)
        if col_off == 0:
            sides_ref[0] = dot(left[2], part).reshape(ROWS, 1, FINE)
        if col_off == 2:
            sides_ref[1] = dot(right[1], part).reshape(ROWS, 1, FINE)
        rows = [left[col_off], left[col_off + 1], right[col_off], right[col_off + 1]]
        total = total + dot(jnp.concatenate(rows, axis=0), part)
    beside_ref[...] = total.reshape(2, 2 * ROWS, FINE)


def conv_sides(before, after, first, last, above, below, weights):
    return pl.pallas_call(
        sides_kernel,
        grid=(1,),
        in_specs=[whole(REACH, ROWS, FINE)] * 4 + [whole(LONG, FINE)] * 2 + [whole(3, 3 * FINE, FINE)],
        out_specs=[whole(2, ROWS, 1, FINE), whole(2, 2 * ROWS, FINE)],
        out_shape=[
            jax.ShapeDtypeStruct((2, ROWS, 1, FINE), F32),
            jax.ShapeDtypeStruct((2, 2 * ROWS, FINE), F32),
        ],
        compiler_params=pltpu.CompilerParams(vmem_limit_bytes=16 * MIB),
    )(before, after, first, last, above, below, in_hbm(weights))


STRIPS = 2
ROW_TILES = COLUMNS // SUBTILE_COLUMNS


def pool_of(group):
    return jnp.where(group == lax.broadcasted_iota(jnp.int32, group.shape, 0), 0.25, 0.0).astype(BF16)


def lifted_of(parts, lift):
    rows = [part.reshape(PX * SLOT, CELLS).astype(BF16) for part in parts]
    return lax.dot_general(
        jnp.concatenate(rows, axis=1), lift, (((0,), (0,)), ((), ())), preferred_element_type=F32
    ).astype(BF16)


def first_of(kept, conv, guidance):
    return (kept.astype(F32) + silu(conv + guidance.astype(F32))).astype(BF16)


def first_kernel(
    here_ref,
    blended_ref,
    blended_beside_ref,
    lift_ref,
    conv_ref,
    cells_ref,
    sides_ref,
    conv_beside_ref,
    before_ref,
    after_ref,
    first_ref,
    pooled_ref,
    pooled_beside_ref,
):
    lift = dot(part_rows(), lift_ref[...]).astype(BF16)
    cell = lax.broadcasted_iota(jnp.int32, (32, CELLS), 1)

    @pl.when(pl.program_id(0) == 0)
    def _():
        pool = pool_of(cell % ROWS // 2)
        both = blended_beside_ref[...].astype(F32)
        lifted = lifted_of([both[:, side * SLOT : (side + 1) * SLOT, :] for side in range(2)], lift)
        kept = [
            jnp.concatenate([before_ref[k] for k in (1, 2)], axis=0),
            jnp.concatenate([after_ref[k] for k in (0, 1)], axis=0),
        ]
        inside = [here_ref[2] > 0, here_ref[2] < PX - 1]
        for side in range(2):
            guidance = lifted[side * CELLS : (side + 1) * CELLS]
            first = first_of(kept[side], conv_beside_ref[side], guidance)
            pooled_beside_ref[side] = jnp.where(inside[side], dot(pool, first), 0.0).astype(BF16)

    row = cell // SUBTILE_COLUMNS
    column = cell % SUBTILE_COLUMNS
    pool = pool_of((row // 2) * 8 + column // 2)
    at = lax.broadcasted_iota(jnp.int32, (STRIP, SUBTILE_COLUMNS, FINE), 1)
    for strip in range(STRIPS):
        parts = []
        for pair in range(ROW_TILES // 2):
            start = (strip * ROW_TILES + 2 * pair) * SLOT
            both = blended_ref[:, start : start + 2 * SLOT, :].astype(F32)
            parts += [both[:, half * SLOT : (half + 1) * SLOT, :] for half in range(2)]
        lifted = lifted_of(parts, lift)
        rows = slice(strip * STRIP, (strip + 1) * STRIP)
        half_rows = slice(strip * STRIP // 2, (strip + 1) * STRIP // 2)
        for tile in range(ROW_TILES):
            columns = slice(tile * SUBTILE_COLUMNS, (tile + 1) * SUBTILE_COLUMNS)
            conv = conv_ref[rows, columns, :].astype(F32)
            if tile == 0:
                conv = conv + jnp.where(at == 0, sides_ref[0, rows], 0.0)
            if tile == ROW_TILES - 1:
                conv = conv + jnp.where(at == SUBTILE_COLUMNS - 1, sides_ref[1, rows], 0.0)
            kept = cells_ref[rows, columns, :].reshape(CELLS, FINE)
            first = first_of(kept, conv.reshape(CELLS, FINE), lifted[tile * CELLS : (tile + 1) * CELLS])
            first_ref[rows, columns, :] = first.reshape(SUBTILE_ROWS, SUBTILE_COLUMNS, FINE)
            pooled = dot(pool, first).reshape(STRIP // 2, 8, FINE).astype(BF16)
            pooled_ref[half_rows, tile * 8 : (tile + 1) * 8, :] = pooled


def first_level(here, blended, lift, conv, cells, sides, conv_beside, before, after):
    count = STRIPS * STRIP
    strip = pl.BlockSpec((count, COLUMNS, FINE), lambda i: (i, 0, 0))
    beside = pl.BlockSpec((PX, 2 * SLOT, CELLS), lambda i: (0, SUBTILES // 2, 0))
    return pl.pallas_call(
        first_kernel,
        grid=(ROWS // count,),
        in_specs=[
            pl.BlockSpec(memory_space=pltpu.SMEM),
            pl.BlockSpec((PX, STRIPS * ROW_TILES * SLOT, CELLS), lambda i: (0, i, 0)),
            beside,
            whole(CHANNELS, FINE),
            strip,
            strip,
            pl.BlockSpec((2, count, 1, FINE), lambda i: (0, i, 0, 0)),
            whole(2, 2 * ROWS, FINE),
            whole(REACH, ROWS, FINE),
            whole(REACH, ROWS, FINE),
        ],
        out_specs=[
            strip,
            pl.BlockSpec((count // 2, COLUMNS // 2, FINE), lambda i: (i, 0, 0)),
            whole(2, ROWS // 2, FINE),
        ],
        out_shape=[
            pltpu.VMEM((ROWS, COLUMNS, FINE), BF16),
            jax.ShapeDtypeStruct((ROWS // 2, COLUMNS // 2, FINE), BF16),
            jax.ShapeDtypeStruct((2, ROWS // 2, FINE), BF16),
        ],
        compiler_params=pltpu.CompilerParams(vmem_limit_bytes=32 * MIB),
    )(here, blended, blended, in_hbm(lift), in_hbm(conv), in_hbm(cells), sides, conv_beside, before, after)


SECOND = 8


def second_kernel(
    pooled_ref, top_ref, bottom_ref, left_ref, right_ref, weights_ref, up_ref, first_ref, out_ref, taps_ref, spread_ref
):
    step = pl.program_id(0)

    @pl.when(step == 0)
    def _():
        fill_all(taps_ref, pooled_ref, top_ref, bottom_ref, left_ref, right_ref)

    second = silu(taps_dot(taps_ref, weights_ref, step * SECOND, SECOND)).astype(BF16)
    projected = dot(second, up_ref[...])
    half = COLUMNS // 2
    for lane in range(FINE // 128):
        part = projected[:, lane * 128 : (lane + 1) * 128]
        for side in range(2):
            spread_ref[lane, pl.ds(side, SECOND * half, stride=2), :] = part
    for lane in range(FINE // 128):
        lanes = slice(lane * 128, (lane + 1) * 128)
        for row in range(SECOND):
            added = spread_ref[lane, row * COLUMNS : (row + 1) * COLUMNS, :]
            for side in range(2):
                first = first_ref[2 * row + side, :, lanes].astype(F32)
                out_ref[2 * row + side, :, lanes] = (first + added).astype(BF16)


def second_level(pooled, halo, weights, up, first):
    strip = pl.BlockSpec((2 * SECOND, COLUMNS, FINE), lambda i: (i, 0, 0))
    return pl.pallas_call(
        second_kernel,
        grid=(ROWS // 2 // SECOND,),
        in_specs=[
            whole(ROWS // 2, COLUMNS // 2, FINE),
            whole(1, COLUMNS // 2, FINE),
            whole(1, COLUMNS // 2, FINE),
            whole(ROWS // 2 + 2, 1, FINE),
            whole(ROWS // 2 + 2, 1, FINE),
            whole(3, 3 * FINE, WIDE),
            whole(WIDE, FINE),
            strip,
        ],
        out_specs=strip,
        out_shape=jax.ShapeDtypeStruct((ROWS, COLUMNS, FINE), BF16),
        scratch_shapes=[
            pltpu.VMEM((ROWS // 2 + 2, COLUMNS // 2, 3 * FINE), BF16),
            pltpu.VMEM((FINE // 128, SECOND * COLUMNS, 128), F32),
        ],
        compiler_params=pltpu.CompilerParams(vmem_limit_bytes=48 * MIB),
    )(pooled, *halo, weights, up, in_vmem(first))


ROWS_AXES = ("z", "core")


def from_rows(last, first):
    down = [(i, i + 1) for i in range(PY - 1)]
    up = [(i + 1, i) for i in range(PY - 1)]
    return lax.ppermute(last, ROWS_AXES, down), lax.ppermute(first, ROWS_AXES, up)


def from_columns(last, first):
    return (
        lax.ppermute(last, "px", [(i, i + 1) for i in range(PX - 1)]),
        lax.ppermute(first, "px", [(i + 1, i) for i in range(PX - 1)]),
    )


def local(
    features,
    coarse,
    send_ids,
    send_counts,
    entry_slot,
    entry_weight_pattern,
    interpolation_weights,
    lift_weight,
    conv_a,
    conv_b,
    up_weight,
):
    here = jnp.stack([lax.axis_index(axis) for axis in ("z", "core", "px")]).astype(jnp.int32)
    outgoing = pack(coarse.transpose(1, 0, 2), send_ids[0].T, send_counts, entry_slot, entry_weight_pattern)
    outgoing, cells = lax.optimization_barrier((outgoing, features))
    own = lax.all_to_all(
        outgoing.reshape(NEAR, OWNED * SLOT, CELLS), ("z", "px"), split_axis=0, concat_axis=0, tiled=True
    )
    weights = conv_a.reshape(3, 3 * FINE, FINE)
    first_columns, last_columns = edge_columns(cells)
    first_columns, last_columns, cells = lax.optimization_barrier((first_columns, last_columns, cells))
    before, after = from_columns(last_columns, first_columns)
    strip = conv_strip(cells, weights)
    own, strip, before, after = lax.optimization_barrier((own, strip, before, after))
    other = lax.ppermute(own, "core", [(0, 1), (1, 0)])
    parts = blend(here, own, other, interpolation_weights)
    parts, strip, before, after = lax.optimization_barrier((parts, strip, before, after))
    blended = lax.all_to_all(parts, "px", split_axis=0, concat_axis=0, tiled=True)

    def long(row):
        rest = jnp.zeros((LONG - COLUMNS - 2 * REACH, FINE), BF16)
        return jnp.concatenate([cells[row], before[:, row], after[:, row], rest], axis=0)

    above, below = from_rows(long(ROWS - 1), long(0))
    conv = conv_inside(cells, above, below, weights, strip)
    sides, conv_beside = conv_sides(before, after, first_columns, last_columns, above, below, weights)
    first, pooled, pooled_beside = first_level(
        here, blended, lift_weight, conv, features, sides, conv_beside, before, after
    )

    def wide(row):
        return jnp.concatenate([pooled[row], pooled_beside[:, row]], axis=0)

    half = COLUMNS // 2
    above, below = from_rows(wide(ROWS // 2 - 1), wide(0))
    columns = [
        jnp.concatenate([above[half + side][None], pooled_beside[side], below[half + side][None]], axis=0)
        for side in range(2)
    ]
    edges = (above[None, :half], below[None, :half], *(column[:, None].astype(F32) for column in columns))
    return second_level(pooled, edges, conv_b.reshape(3, 3 * FINE, WIDE), up_weight, first)


def solution(mesh):
    split = Mesh(mesh.devices.reshape(Z, CORES, PX), ("z", "core", "px"))
    every = ("z", "core", "px")
    placed = (
        P(ROWS_AXES, "px", None),
        P(every, None, None),
        P(every, None, None),
        P(every, None),
        P(every, None),
        P(every, None),
        P(),
        P(),
        P(),
        P(),
        P(),
    )
    return jax.shard_map(
        local, mesh=split, in_specs=placed, out_specs=P(ROWS_AXES, "px", None), check_vma=False
    )
```
